128 devices in a mesh: query: 8 (over y, core), space: 16 (over x, z).
Axes of the slice: x: 4, y: 4, z: 4, core: 2. Of those that a mesh axis runs over, the one named last changes fastest.
Arguments:
- queries: bfloat16 [4096, 256], P('query'), may hold values from -34 to 34
- features: bfloat16 [131072, 256], P(('space', 'query')), may hold values from -6 to 6
- block_lists: int32 [64, 46], replicated, may hold values from 0 to 1023, as said below
- w_query: bfloat16 [256, 256], replicated, may hold values from -1 to 1
- w_key: bfloat16 [256, 256], replicated, may hold values from -0.375 to 0.375
- w_value: bfloat16 [256, 256], replicated, may hold values from -0.375 to 0.375
- w_out: bfloat16 [256, 256], replicated, may hold values from -0.375 to 0.375
- norm_gain: float32 [256], replicated, may hold values from 0.1 to 1.9
- w_mask: bfloat16 [256, 256], replicated, may hold values from -0.375 to 0.375
Outputs:
- new_queries: bfloat16 [4096, 256], P('query')
- mask_logits: float32 [4096, 131072], P('query', 'space')
The draws below stay inside these ranges and needn't reach their ends.
Inputs may be any that keep to these rules, and one draw needn't show every extreme that they name: `block_lists`: each row names 46 distinct superpoint blocks, of which exactly 16 lie on one space index (block g lies on index g // 64) and exactly 2 on each other index; among the 8 rows k * 8 to k * 8 + 7, for k from 1 to 7, these busiest indices are all different.
All inputs are finite; a program needn't handle non-finite values.
Results may differ from the reference program's by a relative error of at most 0.012.
Values may be sent and summed in bfloat16 or wider, within the bound.
No kernel may reach another device: no remote copies, remote signals or barrier semaphores. Data moves between devices by JAX's collectives and lax.ppermute only.
A program may use at most 128 MiB of HBM per device.

```python
import math
import jax
import jax.numpy as jnp
from jax import lax

D = 256
H = 8
HD = 32
QBLK = 64
QBD = 8
SBLK = 128
CAP = 16
REST = 2
OWNERS = 16
GROUPS = 8
L = 46
NQB = 64
Q = 4096
S = 131072
BPD = 64
N_QUERY = 8


def draw_queries(key, part):
    key = jax.random.fold_in(key, 5)
    base_key = jax.random.fold_in(key, 0)
    values = jnp.clip(jax.random.normal(base_key, (Q, D), jnp.float32), -6.0, 6.0)
    return values.astype(jnp.bfloat16)


def draw_block_lists(key, part):
    key = jax.random.fold_in(key, 11)
    hot_key, local_key, shuffle_key = jax.random.split(key, 3)
    busiest = jax.vmap(lambda entry: jax.random.permutation(entry, OWNERS)[:QBD])(jax.random.split(hot_key, GROUPS)).reshape(NQB)
    local_perm = jax.vmap(lambda entry: jax.random.permutation(entry, BPD))(jax.random.split(local_key, NQB))
    rows = jnp.arange(NQB, dtype=jnp.int32)[:, None]
    target = jnp.where(rows == 0, 0, BPD - 1).astype(jnp.int32)
    first = local_perm[:, :1]
    swapped = jnp.where(local_perm == target, first, local_perm)
    columns = jnp.arange(BPD, dtype=jnp.int32)[None, :]
    swapped = jnp.where(columns == 0, target, swapped)
    local_perm = jnp.where(rows < 2, swapped, local_perm).astype(jnp.int32)
    places = jnp.arange(L, dtype=jnp.int32)
    beyond = jnp.maximum(places - CAP, 0)
    offset = jnp.where(places < CAP, 0, 1 + beyond // REST)
    within = jnp.where(places < CAP, places, beyond % REST)
    owner = (busiest[:, None] + offset[None, :]) % OWNERS
    owner = jnp.where(rows == 0, (owner - busiest[:1, None]) % OWNERS, owner)
    owner = jnp.where(rows == 1, (owner - busiest[1:2, None] - 1) % OWNERS, owner)
    local = jnp.take_along_axis(local_perm, jnp.broadcast_to(within[None, :], (NQB, L)), 1)
    listed = owner * BPD + local
    shuffle = jax.vmap(lambda entry: jax.random.permutation(entry, L))(jax.random.split(shuffle_key, NQB))
    return jnp.take_along_axis(listed, shuffle, 1).astype(jnp.int32)


def steps_of(key, extent, pieces, smallest, largest):
    def one(dim, shards_of):
        steps = jax.random.uniform(jax.random.fold_in(jax.random.fold_in(key, 6), dim), (shards_of,), jnp.float32, smallest / len(pieces), largest / len(pieces))
        return jnp.repeat(jnp.exp(steps), extent[dim] // shards_of).reshape((-1,) + (1,) * (len(extent) - dim - 1))

    factor_of = one(*pieces[0])
    for cut in pieces[1:]:
        factor_of = factor_of * one(*cut)
    return factor_of


def gaussian(rng, shape, scale, most, pieces=(), held_as=jnp.bfloat16):
    entries = scale * jax.random.normal(rng, shape, jnp.float32)
    if pieces:
        entries = entries * steps_of(rng, shape, pieces, -0.22, 0.18)
    return jnp.clip(entries, -most, most).astype(held_as)


def setup_inputs(seed: int = 0) -> dict:
    key_list = jax.random.split(jax.random.key(seed), 10)
    queries = draw_queries(jax.random.fold_in(key_list[9], 71), 0)
    features = gaussian(key_list[1], (S, D), 1.0, 6.0, ((0, 128),))
    block_lists = draw_block_lists(jax.random.fold_in(key_list[9], 71), 0)
    w_query = gaussian(key_list[3], (D, D), HD ** -0.5, 1.0)
    w_key = gaussian(key_list[4], (D, D), D ** -0.5, 0.375)
    w_value = gaussian(key_list[5], (D, D), D ** -0.5, 0.375)
    w_out = gaussian(key_list[6], (D, D), D ** -0.5, 0.375)
    norm_gain = jnp.clip(1.0 + 0.18 * jax.random.normal(key_list[7], (D,), jnp.float32), 0.1, 1.9)
    w_mask = gaussian(key_list[8], (D, D), D ** -0.5, 0.375)
    return dict(queries=queries, features=features, block_lists=block_lists, w_query=w_query, w_key=w_key, w_value=w_value, w_out=w_out, norm_gain=norm_gain, w_mask=w_mask)


def layer_norm(rows, gain):
    center = rows - lax.optimization_barrier(jnp.mean(rows, axis=-1, keepdims=True))
    spread = lax.optimization_barrier(jnp.mean(center * center, axis=-1, keepdims=True))
    return center * lax.rsqrt(spread + 1e-05) * gain

def reference(queries, features, block_lists, w_query, w_key, w_value, w_out, norm_gain, w_mask):
    score_scale = 1.0 / math.sqrt(HD)
    query_proj = jnp.dot(queries, w_query, preferred_element_type=jnp.float32).astype(jnp.bfloat16)
    key_rows = jnp.dot(features, w_key, preferred_element_type=jnp.float32).astype(jnp.bfloat16)
    value_rows = jnp.dot(features, w_value, preferred_element_type=jnp.float32).astype(jnp.bfloat16)
    key_blocks = key_rows.reshape(S // SBLK, SBLK, D)
    value_blocks = value_rows.reshape(S // SBLK, SBLK, D)

    def attend(item):
        query_block, listed = item
        picked_keys = key_blocks[listed].reshape(L * SBLK, H, HD).astype(jnp.float32)
        picked_values = value_blocks[listed].reshape(L * SBLK, H, HD).astype(jnp.float32)
        heads = query_block.reshape(QBLK, H, HD).astype(jnp.float32)
        scores = jnp.einsum('qhd,khd->hqk', heads, picked_keys, precision=lax.Precision.HIGHEST) * score_scale
        highest = lax.optimization_barrier(jnp.max(scores, axis=-1, keepdims=True))
        numerators = jnp.exp(scores - highest)
        totals = lax.optimization_barrier(jnp.sum(numerators, axis=-1))
        rounded_weights = numerators.astype(jnp.bfloat16).astype(jnp.float32)
        mixed = jnp.einsum('hqk,khd->qhd', rounded_weights, picked_values, precision=lax.Precision.HIGHEST)
        return (mixed / jnp.transpose(totals)[:, :, None]).reshape(QBLK, D).astype(jnp.bfloat16)
    attended = lax.map(attend, (query_proj.reshape(NQB, QBLK, D), block_lists)).reshape(Q, D)
    residual = queries.astype(jnp.float32) + jnp.dot(attended, w_out, preferred_element_type=jnp.float32)
    new_queries = layer_norm(residual, norm_gain).astype(jnp.bfloat16)
    mask_embed = jnp.dot(new_queries, w_mask, preferred_element_type=jnp.float32).astype(jnp.bfloat16)
    mask_scale = 1.0 / math.sqrt(D)

    def logits_rows(rows):
        return jnp.dot(rows, features.T, preferred_element_type=jnp.float32) * mask_scale
    mask_logits = lax.map(logits_rows, mask_embed.reshape(N_QUERY, QBD * QBLK, D)).reshape(Q, S)
    return (new_queries, mask_logits)
```

```python
import functools
import math

import jax
import jax.numpy as jnp
from jax import lax
from jax.experimental import pallas as pl
from jax.experimental.pallas import tpu as pltpu
from jax.sharding import PartitionSpec as P

D = 256
H = 8
HD = 32
QBLK = 64
SBLK = 128
CAP = 16
LOG2E = math.log2(math.e)
BF16 = jnp.bfloat16
F32 = jnp.float32
NT = (((1,), (1,)), ((), ()))
TN = (((0,), (0,)), ((), ()))
TAIL = 128
CHIPS = 4
OWN_BLOCKS = 8
SHARD_BLOCKS = 2 * CHIPS * OWN_BLOCKS
PHASES = 3
WIDTH = 20
COUNTS = PHASES * WIDTH
PAIRS = H // 2
WIDE = 2 * QBLK
MIB = 1024 * 1024
IN_SMEM = pl.BlockSpec(memory_space=pltpu.SMEM)
IN_VMEM = pl.BlockSpec(memory_space=pltpu.VMEM)
IN_HBM = pl.BlockSpec(memory_space=pltpu.HBM)


def head_of_lane(shape):
    return lax.broadcasted_iota(jnp.int32, shape, len(shape) - 1) // HD


def local_lists(place_ref, lists):
    chip, core = lax.div(place_ref[0], 2), lax.rem(place_ref[0], 2)
    inside = lax.rem(lists, OWN_BLOCKS)
    device = lax.rem(lax.div(lists, OWN_BLOCKS), 2 * CHIPS)
    other = jnp.where(lax.rem(device, 2) == core, 0, 1)
    ahead = lax.rem(lax.div(device, 2) - chip + CHIPS, CHIPS)
    near = jnp.where(ahead == 1, 2, 0) * OWN_BLOCKS + other * OWN_BLOCKS + inside
    half = OWN_BLOCKS // 2
    far = lax.div(inside, half) * OWN_BLOCKS + other * half + lax.rem(inside, half)
    position = jnp.where(ahead == 2, far, near)
    phase = jnp.where(ahead == 0, 0, jnp.where(ahead == 2, 2, 1))
    phase = jnp.where(lax.div(lists, SHARD_BLOCKS) == place_ref[1], phase, -1)
    width = lists.shape[0]
    row = lax.broadcasted_iota(jnp.int32, (width, width), 0)
    column = lax.broadcasted_iota(jnp.int32, (width, width), 1)
    earlier = jnp.where(column < row, 1.0, 0.0).astype(BF16)
    code = jnp.full(lists.shape, -1.0, F32)
    for p in range(PHASES):
        mine = phase == p
        rank = jnp.dot(earlier, jnp.where(mine, 1.0, 0.0).astype(BF16), preferred_element_type=F32)
        code = jnp.where(mine, (p * WIDTH + rank) * 128.0 + position.astype(F32), code)
    return code


def project_kernel(place_ref, lists_ref, queries_ref, wq_ref, wk_ref, out_ref, ids_ref, lists, queries, wq, wk, ids, sems):
    blocks = out_ref.shape[0]
    copies = [
        pltpu.make_async_copy(source, target, sems.at[i])
        for i, (source, target) in enumerate(
            [(lists_ref, lists), (queries_ref, queries), (wq_ref, wq), (wk_ref, wk)]
        )
    ]
    for copy in copies:
        copy.start()
    copies[0].wait()
    code = local_lists(place_ref, lists[...])
    list_row = lax.broadcasted_iota(jnp.int32, code.shape, 1)
    lane = lax.broadcasted_iota(jnp.int32, (code.shape[0], 128), 1)
    for b in range(blocks):
        wanted = place_ref[0] * blocks + b
        mine = jnp.sum(jnp.where(list_row == wanted, code, 0.0), axis=1, keepdims=True).astype(jnp.int32)
        slot = jnp.where(mine < 0, -1, lax.div(mine, 128))
        found = jnp.where(slot == lane, lax.rem(mine, 128), 0)
        phase = jnp.where(slot < 0, -1, lax.div(slot, WIDTH))
        found = found + jnp.where(phase == lane - COUNTS, jnp.where(phase < 0, 0, 1), 0)
        ids[b : b + 1, :] = jnp.sum(found.astype(F32), axis=0, keepdims=True).astype(jnp.int32)
    tell = pltpu.make_async_copy(ids, ids_ref, sems.at[4])
    tell.start()
    for copy in copies[1:]:
        copy.wait()
    proj = jnp.dot(queries[...], wq[...], preferred_element_type=F32).astype(BF16)
    head = head_of_lane((QBLK, D))
    scale = LOG2E / math.sqrt(HD)
    none = jnp.zeros((QBLK, D), BF16)
    for b in range(blocks):
        rows = proj[b * QBLK : (b + 1) * QBLK]
        for c in range(PAIRS):
            two = [jnp.where(head == h, rows, none) for h in (2 * c, 2 * c + 1)]
            folded = lax.dot_general(wk[...], jnp.concatenate(two, axis=0), NT, preferred_element_type=F32)
            out_ref[b, :, c * WIDE : (c + 1) * WIDE] = (folded * scale).astype(BF16)
    tell.wait()


def project(place, lists, queries, w_query, w_key):
    blocks = queries.shape[0] // QBLK
    return pl.pallas_call(
        project_kernel,
        out_shape=(
            jax.ShapeDtypeStruct((blocks, D, H * QBLK), BF16),
            jax.ShapeDtypeStruct((blocks, 128), jnp.int32),
        ),
        in_specs=[IN_SMEM] + [IN_HBM] * 4,
        out_specs=(IN_VMEM, IN_SMEM),
        scratch_shapes=[
            pltpu.VMEM(lists.shape, jnp.int32),
            pltpu.VMEM(queries.shape, BF16),
            pltpu.VMEM((D, D), BF16),
            pltpu.VMEM((D, D), BF16),
            pltpu.VMEM((blocks, 128), jnp.int32),
            pltpu.SemaphoreType.DMA((5,)),
        ],
        compiler_params=pltpu.CompilerParams(vmem_limit_bytes=16 * MIB),
        cost_estimate=pl.CostEstimate(
            flops=2 * queries.shape[0] * D * D * (H + 1), bytes_accessed=3 * MIB, transcendentals=0
        ),
        name="project",
    )(place, lists, queries, w_query, w_key)


def score(item, items, feats, q_ref, scores):
    keys = [feats[pl.ds(pl.multiple_of(items[item, 1 + k], SBLK), SBLK), :] for k in range(2)]
    scores[...] = jnp.dot(jnp.concatenate(keys, axis=0), q_ref[items[item, 3]], preferred_element_type=F32)


def weigh(item, items, feats, scores, acc, stats):
    b = items[item, 0]
    keys = [feats[pl.ds(pl.multiple_of(items[item, 1 + k], SBLK), SBLK), :] for k in range(2)]
    turned = jnp.concatenate(keys, axis=0).T
    alone = items[item, 4] == 1
    halves = H * QBLK // 2
    for c in range(2):
        part = slice(c * halves, (c + 1) * halves)
        first = scores[:SBLK, part]
        second = jnp.where(alone, -jnp.inf, scores[SBLK:, part])
        top = stats[b, 0:1, part]
        higher = jnp.maximum(top, jnp.max(jnp.maximum(first, second), axis=0, keepdims=True))
        factor = jnp.exp2(top - higher)
        first = jnp.exp2(first - higher)
        second = jnp.exp2(second - higher)
        stats[b, 0:1, part] = higher
        stats[b, 1:2, part] = stats[b, 1:2, part] * factor + jnp.sum(first + second, axis=0, keepdims=True)
        weights = jnp.concatenate([first.astype(BF16), second.astype(BF16)], axis=0)
        acc[b, :, part] = acc[b, :, part] * factor + jnp.dot(turned, weights, preferred_element_type=F32)


def attend_kernel(phase, sizes, last, ids_ref, q_ref, *rest):
    count = len(sizes)
    piece_refs, rest = rest[:count], rest[count:]
    if phase:
        rest = rest[2:]
    if last:
        wv_ref, rest = rest[0], rest[1:]
        acc, stats_ref, out_ref, feats, items, even, odd, wv, sems = rest
        load = pltpu.make_async_copy(wv_ref, wv, sems.at[0])
        load.start()
    else:
        acc, stats_ref, feats, items, even, odd, sems = rest
    held = 0
    for i, (size, ref) in enumerate(zip(sizes, piece_refs)):
        if phase == 0 and i == 0:
            own = pltpu.make_async_copy(ref, feats.at[pl.ds(held, size)], sems.at[1])
            own.start()
        else:
            feats[held : held + size, :] = ref[...]
        held += size
    blocks = q_ref.shape[0]

    def put(at, b, first, second, query, alone):
        for k, value in enumerate((b, first, second, query, alone)):
            items[at, k] = value

    def one_block(b, held):
        found = ids_ref[b, COUNTS + phase]

        def one(i, held):
            first = ids_ref[b, phase * WIDTH + 2 * i] * SBLK
            alone = 2 * i + 1 >= found
            second = jnp.where(alone, first, ids_ref[b, phase * WIDTH + 2 * i + 1] * SBLK)
            put(held, b, first, second, b, jnp.where(alone, 1, 0))
            return held + 1

        return lax.fori_loop(0, lax.div(found + 1, 2), one, held)

    total_items = lax.fori_loop(0, blocks, one_block, 0)
    for k in range(2):
        put(total_items + k, blocks, 0, 0, 0, 0)
    if phase == 0:
        acc[...] = jnp.zeros(acc.shape, F32)
        stats_ref[:, 0:1, :] = jnp.full((acc.shape[0], 1, H * QBLK), -jnp.inf, F32)
        stats_ref[:, 1:2, :] = jnp.zeros((acc.shape[0], 1, H * QBLK), F32)
        own.wait()
    score(0, items, feats, q_ref, even)

    def two_items(i, carry):
        score(2 * i + 1, items, feats, q_ref, odd)
        weigh(2 * i, items, feats, even, acc, stats_ref)
        score(2 * i + 2, items, feats, q_ref, even)
        weigh(2 * i + 1, items, feats, odd, acc, stats_ref)
        return carry

    lax.fori_loop(0, lax.div(total_items + 1, 2), two_items, 0)
    if not last:
        return
    load.wait()
    wv_t = wv[...].T
    slot = lax.broadcasted_iota(jnp.int32, (16, WIDE), 0)
    column = lax.broadcasted_iota(jnp.int32, (QBLK, D + TAIL), 1)
    odd_head = jnp.where(column < D, lax.rem(lax.div(column, HD), 2), lax.rem(lax.div(column, 16), 2))
    empty = jnp.zeros((TAIL - 32, WIDE), F32)
    for b in range(q_ref.shape[0]):
        diagonal = []
        tail = jnp.zeros((16, WIDE), F32)
        for c in range(PAIRS):
            part = slice(c * WIDE, (c + 1) * WIDE)
            total = stats_ref[b, 1:2, part]
            mean = (acc[b, :, part] * (1.0 / total)).astype(BF16)
            heads = slice(2 * HD * c, 2 * HD * (c + 1))
            diagonal.append(jnp.dot(wv_t[heads], mean, preferred_element_type=F32))
            level = stats_ref[b, 0:1, part] + jnp.log(total) * LOG2E
            for piece in range(3):
                rounded = level.astype(BF16).astype(F32)
                level = level - rounded
                tail = jnp.where(slot == piece * PAIRS + c, rounded, tail)
        turned = jnp.concatenate(diagonal + [tail, tail, empty], axis=0).T
        rows = jnp.where(odd_head == 1, turned[QBLK:], turned[:QBLK])
        out_ref[b * QBLK : (b + 1) * QBLK, :] = rows.astype(BF16)


def attend(phase, ids, folded, arrays, state, w_value):
    blocks = folded.shape[0]
    last = w_value is not None
    sizes = [a.shape[0] for a in arrays]
    out_shape = [
        jax.ShapeDtypeStruct((blocks + 1, D, H * QBLK), F32),
        jax.ShapeDtypeStruct((blocks + 1, 8, H * QBLK), F32),
    ]
    args = [ids, folded, *arrays]
    in_specs = [IN_SMEM, IN_VMEM] + [IN_VMEM] * len(arrays)
    most = blocks * (CAP // 2 + 1) + 2
    scratch = [pltpu.VMEM((sum(sizes), D), BF16), pltpu.SMEM((most, 8), jnp.int32)]
    scratch += [pltpu.VMEM((2 * SBLK, H * QBLK), F32)] * 2
    aliases = {}
    if phase == 0:
        in_specs[2] = IN_HBM
    else:
        aliases = {len(args): 0, len(args) + 1: 1}
        args += list(state)
        in_specs += [IN_VMEM] * 2
    if last:
        args.append(w_value)
        in_specs.append(IN_HBM)
        out_shape.append(jax.ShapeDtypeStruct((blocks * QBLK, D + TAIL), BF16))
        scratch.append(pltpu.VMEM((D, D), BF16))
    return pl.pallas_call(
        functools.partial(attend_kernel, phase, sizes, last),
        out_shape=out_shape,
        in_specs=in_specs,
        out_specs=[IN_VMEM] * len(out_shape),
        input_output_aliases=aliases,
        scratch_shapes=scratch + [pltpu.SemaphoreType.DMA((2,))],
        compiler_params=pltpu.CompilerParams(vmem_limit_bytes=16 * MIB),
        cost_estimate=pl.CostEstimate(flops=1_000_000_000, bytes_accessed=4 * MIB, transcendentals=700_000),
        name="attend_%d" % phase,
    )(*args)


def finish_kernel(place_ref, got_ref, queries_ref, wo_ref, gain_ref, out_ref, queries, wo, gain, sems):
    sources, count, _ = got_ref.shape
    first = pl.multiple_of(place_ref[1] * count, count)
    copies = [
        pltpu.make_async_copy(queries_ref.at[pl.ds(first, count)], queries, sems.at[0]),
        pltpu.make_async_copy(wo_ref, wo, sems.at[1]),
        pltpu.make_async_copy(gain_ref, gain, sems.at[2]),
    ]
    for copy in copies:
        copy.start()
    slot = lax.broadcasted_iota(jnp.int32, (TAIL, D), 0)
    pairs = H // 2
    head = 2 * lax.rem(slot, pairs) + lax.div(slot, 16)
    spread = (head == head_of_lane((TAIL, D))) & (lax.rem(slot, 16) < 3 * pairs) & (slot < 32)
    spread = jnp.where(spread, 1.0, 0.0).astype(BF16)
    tails = got_ref[:, :, D:].reshape(sources * count, TAIL)
    levels = jnp.dot(tails, spread, preferred_element_type=F32).reshape(sources, count, D)
    factors = jnp.exp2(levels - jnp.max(levels, axis=0, keepdims=True))
    mixed = jnp.sum(factors * got_ref[:, :, :D].astype(F32), axis=0)
    attended = (mixed / jnp.sum(factors, axis=0)).astype(BF16)
    for copy in copies:
        copy.wait()
    rows = queries[...].astype(F32) + jnp.dot(attended, wo[...], preferred_element_type=F32)
    center = rows - jnp.mean(rows, axis=1, keepdims=True)
    variance = jnp.mean(center * center, axis=1, keepdims=True)
    updated = (center * lax.rsqrt(variance + 1e-05) * gain[...]).astype(BF16)
    for i in range(sources):
        out_ref[i] = updated


def finish(place, got, queries, w_out, norm_gain):
    sources, count, _ = got.shape
    return pl.pallas_call(
        finish_kernel,
        out_shape=jax.ShapeDtypeStruct((sources, count, D), BF16),
        in_specs=[IN_SMEM, IN_VMEM] + [IN_HBM] * 3,
        out_specs=IN_VMEM,
        scratch_shapes=[
            pltpu.VMEM((count, D), BF16),
            pltpu.VMEM((D, D), BF16),
            pltpu.VMEM((1, D), F32),
            pltpu.SemaphoreType.DMA((3,)),
        ],
        compiler_params=pltpu.CompilerParams(vmem_limit_bytes=16 * MIB),
        cost_estimate=pl.CostEstimate(flops=10_000_000, bytes_accessed=MIB, transcendentals=140_000),
        name="finish",
    )(place, got, queries, w_out, norm_gain.reshape(1, D))


STEP = 512
SLOTS = 4


def piece_row(place_ref, piece):
    ahead, other, row = piece
    index = place_ref[0]
    chip = lax.rem(lax.div(index, 2) + ahead + CHIPS, CHIPS)
    core = lax.rem(index, 2)
    core = 1 - core if other else core
    return (chip * 2 + core) * (OWN_BLOCKS * SBLK) + row


def logits_kernel(pieces, place_ref, updated_ref, wm_ref, own_ref, *rest):
    count = len(pieces)
    piece_refs = rest[: count - 1]
    updated_out, out_ref, embed, wm, own, tiles, in_sems, out_sems = rest[count - 1 :]
    load_wm = pltpu.make_async_copy(wm_ref, wm, in_sems.at[0])
    load_wm.start()
    load_own = pltpu.make_async_copy(own_ref, own, in_sems.at[1])
    load_own.start()
    keep = pltpu.make_async_copy(updated_ref, updated_out, in_sems.at[2])
    keep.start()
    load_wm.wait()
    rows = jnp.dot(updated_ref[...], wm[...], preferred_element_type=F32).astype(BF16)
    embed[...] = rows * (1.0 / math.sqrt(D))
    stores = []
    for i, ref in [*enumerate(piece_refs, 1), (0, own)]:
        if i == 0:
            load_own.wait()
        for row in range(0, ref.shape[0], STEP):
            slot = len(stores) % SLOTS
            if len(stores) >= SLOTS:
                stores[-SLOTS].wait()
            tiles[slot] = lax.dot_general(
                embed[...], ref[row : row + STEP, :], NT, preferred_element_type=F32
            )
            column = pl.multiple_of(piece_row(place_ref, pieces[i]) + row, STEP)
            stores.append(
                pltpu.make_async_copy(tiles.at[slot], out_ref.at[:, pl.ds(column, STEP)], out_sems.at[slot])
            )
            stores[-1].start()
    for store in stores[-SLOTS:]:
        store.wait()
    keep.wait()


def logits(place, updated, w_mask, pieces, arrays):
    count = updated.shape[0]
    shard = sum(a.shape[0] for a in arrays)
    return pl.pallas_call(
        functools.partial(logits_kernel, pieces),
        out_shape=(
            jax.ShapeDtypeStruct(updated.shape, BF16),
            jax.ShapeDtypeStruct((count, shard), F32),
        ),
        in_specs=[IN_SMEM, IN_VMEM, IN_HBM, IN_HBM] + [IN_VMEM] * (len(arrays) - 1),
        out_specs=(IN_HBM, IN_HBM),
        scratch_shapes=[
            pltpu.VMEM((count, D), BF16),
            pltpu.VMEM((D, D), BF16),
            pltpu.VMEM(arrays[0].shape, BF16),
            pltpu.VMEM((SLOTS, count, STEP), F32),
            pltpu.SemaphoreType.DMA((3,)),
            pltpu.SemaphoreType.DMA((SLOTS,)),
        ],
        compiler_params=pltpu.CompilerParams(vmem_limit_bytes=16 * MIB),
        cost_estimate=pl.CostEstimate(
            flops=2 * count * shard * D, bytes_accessed=20 * MIB, transcendentals=0
        ),
        name="logits",
    )(place, updated, w_mask, *arrays)


def shards(queries, features, block_lists, w_query, w_key, w_value, w_out, norm_gain, w_mask):
    space = lax.axis_size("space")
    place = jnp.stack([lax.axis_index("query"), lax.axis_index("space")]).astype(jnp.int32)
    up = [(y * 2 + c, (y + 1) % CHIPS * 2 + c) for y in range(CHIPS) for c in range(2)]
    down = [(y * 2 + c, (y - 1) % CHIPS * 2 + c) for y in range(CHIPS) for c in range(2)]
    cores = [(i, i ^ 1) for i in range(2 * CHIPS)]

    def send(rows, pairs):
        return lax.ppermute(rows, "query", pairs)

    below = send(features, up)
    above = send(features, down)
    beside = send(features, cores)
    folded, ids = project(place, block_lists.T, queries, w_query, w_key)
    state = attend(0, ids, folded, [features, beside], None, None)
    below, above, state = lax.optimization_barrier((below, above, tuple(state)))
    half = features.shape[0] // 2
    far_low = send(below[:half], up)
    far_high = send(above[half:], down)
    near = [below, send(below, cores), above, send(above, cores)]
    state = attend(1, ids, folded, near, state, None)
    far_low, far_high, state = lax.optimization_barrier((far_low, far_high, tuple(state)))
    far = [far_low, send(far_low, cores), far_high, send(far_high, cores)]
    partial = attend(2, ids, folded, far, state, w_value)[2]

    count = queries.shape[0] // space
    got = lax.all_to_all(partial.reshape(space, count, D + TAIL), "space", 0, 0)
    mine = finish(place, got, queries, w_out, norm_gain)
    updated = lax.all_to_all(mine, "space", 0, 0).reshape(queries.shape)
    pieces = [(0, False, 0), (0, True, 0), (-1, False, 0), (-1, True, 0), (1, False, 0), (1, True, 0)]
    pieces += [(-2, False, 0), (-2, True, 0), (2, False, half), (2, True, half)]
    return logits(place, updated, w_mask, pieces, [features, beside, *near, *far])


def solution(mesh):
    placed = (P("query", None), P(("space", "query"), None), P(), P(), P(), P(), P(), P(), P())
    return jax.shard_map(
        shards,
        mesh=mesh,
        in_specs=placed,
        out_specs=(P("query", None), P("query", "space")),
        check_vma=False,
    )
```

```python
import functools
import math

import jax
import jax.numpy as jnp
from jax import lax
from jax.experimental import pallas as pl
from jax.experimental.pallas import tpu as pltpu
from jax.sharding import PartitionSpec as P

D = 256
H = 8
HD = 32
QBLK = 64
SBLK = 128
CAP = 16
LOG2E = math.log2(math.e)
BF16 = jnp.bfloat16
F32 = jnp.float32
NT = (((1,), (1,)), ((), ()))
TN = (((0,), (0,)), ((), ()))
TAIL = 128
CHIPS = 4
OWN_BLOCKS = 8
SHARD_BLOCKS = 2 * CHIPS * OWN_BLOCKS
PHASES = 3
WIDTH = 20
LAST = 127
COUNTS = PHASES * WIDTH
PAIRS = H // 2
WIDE = 2 * QBLK
MIB = 1024 * 1024
IN_SMEM = pl.BlockSpec(memory_space=pltpu.SMEM)
IN_VMEM = pl.BlockSpec(memory_space=pltpu.VMEM)
IN_HBM = pl.BlockSpec(memory_space=pltpu.HBM)


def stay(array):
    return pltpu.with_memory_space_constraint(array, pltpu.HBM)


def head_of_lane(shape):
    return lax.broadcasted_iota(jnp.int32, shape, len(shape) - 1) // HD


def local_lists(place_ref, lists):
    chip, core = lax.div(place_ref[0], 2), lax.rem(place_ref[0], 2)
    inside = lax.rem(lists, OWN_BLOCKS)
    device = lax.rem(lax.div(lists, OWN_BLOCKS), 2 * CHIPS)
    other = jnp.where(lax.rem(device, 2) == core, 0, 1)
    ahead = lax.rem(lax.div(device, 2) - chip + CHIPS, CHIPS)
    near = jnp.where(ahead == 1, 2, 0) * OWN_BLOCKS + other * OWN_BLOCKS + inside
    half = OWN_BLOCKS // 2
    far = lax.div(inside, half) * OWN_BLOCKS + other * half + lax.rem(inside, half)
    position = jnp.where(ahead == 2, far, near)
    phase = jnp.where(ahead == 0, 0, jnp.where(ahead == 2, 2, 1))
    phase = jnp.where(lax.div(lists, SHARD_BLOCKS) == place_ref[1], phase, -1)
    width = lists.shape[0]
    row = lax.broadcasted_iota(jnp.int32, (width, width), 0)
    column = lax.broadcasted_iota(jnp.int32, (width, width), 1)
    earlier = jnp.where(column < row, 1.0, 0.0).astype(BF16)
    code = jnp.full(lists.shape, -1.0, F32)
    for p in range(PHASES):
        mine = phase == p
        rank = jnp.dot(earlier, jnp.where(mine, 1.0, 0.0).astype(BF16), preferred_element_type=F32)
        code = jnp.where(mine, (p * WIDTH + rank) * 128.0 + position.astype(F32), code)
    return code


def write_items(ids, items, blocks):
    for phase in range(PHASES):

        def one_block(b, held):
            found = ids[b, COUNTS + phase]

            def one(i, held):
                first = ids[b, phase * WIDTH + 2 * i]
                alone = 2 * i + 1 >= found
                second = jnp.where(alone, first, ids[b, phase * WIDTH + 2 * i + 1])
                items[phase, held] = ((jnp.where(alone, 1, 0) * 64 + second) * 64 + first) * 16 + b
                return held + 1

            return lax.fori_loop(0, lax.div(found + 1, 2), one, held)

        total = lax.fori_loop(0, blocks, one_block, 0)
        items[phase, total] = blocks
        items[phase, total + 1] = blocks
        items[phase, LAST] = total


def project_kernel(place_ref, *refs):
    sources, rest = refs[:9], refs[9:]
    out_ref, items, wv_t, wo, gain, wm, own, mine, rest = *rest[:8], rest[8:]
    lists, queries, wq, wk, wv, ids, ids_smem, sems = rest
    blocks = out_ref.shape[0]
    count = mine.shape[0]
    lists_ref, queries_ref, wq_ref, wk_ref, wv_ref, wo_ref, gain_ref, wm_ref, own_ref = sources
    mine_ref = queries_ref.at[pl.ds(pl.multiple_of(place_ref[1] * count, count), count)]
    moves = [(lists_ref, lists), (queries_ref, queries), (wq_ref, wq), (wk_ref, wk), (wv_ref, wv)]
    moves += [(wo_ref, wo), (gain_ref, gain), (wm_ref, wm), (own_ref, own), (mine_ref, mine)]
    copies = [pltpu.make_async_copy(source, target, sems.at[i]) for i, (source, target) in enumerate(moves)]
    for copy in copies:
        copy.start()
    copies[0].wait()
    code = local_lists(place_ref, lists[...])
    list_row = lax.broadcasted_iota(jnp.int32, code.shape, 1)
    lane = lax.broadcasted_iota(jnp.int32, (code.shape[0], 128), 1)
    for b in range(blocks):
        wanted = place_ref[0] * blocks + b
        listed = jnp.sum(jnp.where(list_row == wanted, code, 0.0), axis=1, keepdims=True).astype(jnp.int32)
        slot = jnp.where(listed < 0, -1, lax.div(listed, 128))
        found = jnp.where(slot == lane, lax.rem(listed, 128), 0)
        phase = jnp.where(slot < 0, -1, lax.div(slot, WIDTH))
        found = found + jnp.where(phase == lane - COUNTS, jnp.where(phase < 0, 0, 1), 0)
        ids[b : b + 1, :] = jnp.sum(found.astype(F32), axis=0, keepdims=True).astype(jnp.int32)
    tell = pltpu.make_async_copy(ids, ids_smem, sems.at[len(moves)])
    tell.start()
    for copy in copies[1:]:
        copy.wait()
    wv_t[...] = wv[...].T
    proj = jnp.dot(queries[...], wq[...], preferred_element_type=F32).astype(BF16)
    head = head_of_lane((QBLK, D))
    scale = LOG2E / math.sqrt(HD)
    none = jnp.zeros((QBLK, D), BF16)
    for b in range(blocks):
        rows = proj[b * QBLK : (b + 1) * QBLK]
        for c in range(PAIRS):
            two = [jnp.where(head == h, rows, none) for h in (2 * c, 2 * c + 1)]
            folded = lax.dot_general(wk[...], jnp.concatenate(two, axis=0), NT, preferred_element_type=F32)
            out_ref[b, :, c * WIDE : (c + 1) * WIDE] = (folded * scale).astype(BF16)
    tell.wait()
    write_items(ids_smem, items, blocks)


def project(place, count, lists, queries, w_query, w_key, w_value, w_out, norm_gain, w_mask, features):
    blocks = queries.shape[0] // QBLK
    square = jax.ShapeDtypeStruct((D, D), BF16)
    gain = norm_gain.reshape(1, D)
    return pl.pallas_call(
        project_kernel,
        out_shape=(
            jax.ShapeDtypeStruct((blocks, D, H * QBLK), BF16),
            jax.ShapeDtypeStruct((8, 128), jnp.int32),
            square,
            square,
            jax.ShapeDtypeStruct(gain.shape, F32),
            square,
            jax.ShapeDtypeStruct(features.shape, BF16),
            jax.ShapeDtypeStruct((count, D), BF16),
        ),
        in_specs=[IN_SMEM] + [IN_HBM] * 9,
        out_specs=(IN_VMEM, IN_SMEM) + (IN_VMEM,) * 6,
        scratch_shapes=[
            pltpu.VMEM(lists.shape, jnp.int32),
            pltpu.VMEM(queries.shape, BF16),
            pltpu.VMEM((D, D), BF16),
            pltpu.VMEM((D, D), BF16),
            pltpu.VMEM((D, D), BF16),
            pltpu.VMEM((blocks, 128), jnp.int32),
            pltpu.SMEM((blocks, 128), jnp.int32),
            pltpu.SemaphoreType.DMA((11,)),
        ],
        compiler_params=pltpu.CompilerParams(vmem_limit_bytes=16 * MIB),
        cost_estimate=pl.CostEstimate(
            flops=2 * queries.shape[0] * D * D * (H + 1), bytes_accessed=3 * MIB, transcendentals=0
        ),
        name="project",
    )(place, *map(stay, (lists, queries, w_query, w_key, w_value, w_out, gain, w_mask, features)))


def keys_of(item, feats):
    rows = [lax.rem(lax.div(item, 16 * step), 64) * SBLK for step in (1, 64)]
    return jnp.concatenate([feats[pl.ds(pl.multiple_of(row, SBLK), SBLK), :] for row in rows], axis=0)


def score(item, feats, q_ref, scores):
    b = jnp.minimum(lax.rem(item, 16), q_ref.shape[0] - 1)
    scores[...] = jnp.dot(keys_of(item, feats), q_ref[b], preferred_element_type=F32)


def weigh(item, feats, scores, acc, stats):
    b = lax.rem(item, 16)
    turned = keys_of(item, feats).T
    alone = lax.div(item, 16 * 64 * 64) == 1
    halves = H * QBLK // 2
    for c in range(2):
        part = slice(c * halves, (c + 1) * halves)
        first = scores[:SBLK, part]
        second = jnp.where(alone, -jnp.inf, scores[SBLK:, part])
        top = stats[b, 0:1, part]
        higher = jnp.maximum(top, jnp.max(jnp.maximum(first, second), axis=0, keepdims=True))
        factor = jnp.exp2(top - higher)
        first = jnp.exp2(first - higher)
        second = jnp.exp2(second - higher)
        stats[b, 0:1, part] = higher
        stats[b, 1:2, part] = stats[b, 1:2, part] * factor + jnp.sum(first + second, axis=0, keepdims=True)
        weights = jnp.concatenate([first.astype(BF16), second.astype(BF16)], axis=0)
        acc[b, :, part] = acc[b, :, part] * factor + jnp.dot(turned, weights, preferred_element_type=F32)


def attend_kernel(phase, sizes, last, items, q_ref, *rest):
    count = len(sizes)
    piece_refs, rest = rest[:count], rest[count:]
    if phase:
        rest = rest[2:]
    if last:
        wv_t, acc, stats_ref, out_ref, feats, even, odd = rest
    else:
        acc, stats_ref, feats, even, odd = rest
    held = 0
    for size, ref in zip(sizes, piece_refs):
        feats[held : held + size, :] = ref[...]
        held += size
    if phase == 0:
        acc[...] = jnp.zeros(acc.shape, F32)
        stats_ref[:, 0:1, :] = jnp.full((acc.shape[0], 1, H * QBLK), -jnp.inf, F32)
        stats_ref[:, 1:2, :] = jnp.zeros((acc.shape[0], 1, H * QBLK), F32)
    score(items[phase, 0], feats, q_ref, even)

    def two_items(i, carry):
        score(items[phase, 2 * i + 1], feats, q_ref, odd)
        weigh(items[phase, 2 * i], feats, even, acc, stats_ref)
        score(items[phase, 2 * i + 2], feats, q_ref, even)
        weigh(items[phase, 2 * i + 1], feats, odd, acc, stats_ref)
        return carry

    lax.fori_loop(0, lax.div(items[phase, LAST] + 1, 2), two_items, 0)
    if not last:
        return
    slot = lax.broadcasted_iota(jnp.int32, (16, WIDE), 0)
    column = lax.broadcasted_iota(jnp.int32, (QBLK, D + TAIL), 1)
    odd_head = jnp.where(column < D, lax.rem(lax.div(column, HD), 2), lax.rem(lax.div(column, 16), 2))
    empty = jnp.zeros((TAIL - 32, WIDE), F32)
    for b in range(q_ref.shape[0]):
        diagonal = []
        tail = jnp.zeros((16, WIDE), F32)
        for c in range(PAIRS):
            part = slice(c * WIDE, (c + 1) * WIDE)
            total = stats_ref[b, 1:2, part]
            mean = (acc[b, :, part] * (1.0 / total)).astype(BF16)
            heads = slice(2 * HD * c, 2 * HD * (c + 1))
            diagonal.append(jnp.dot(wv_t[heads, :], mean, preferred_element_type=F32))
            level = stats_ref[b, 0:1, part] + jnp.log(total) * LOG2E
            for piece in range(3):
                rounded = level.astype(BF16).astype(F32)
                level = level - rounded
                tail = jnp.where(slot == piece * PAIRS + c, rounded, tail)
        turned = jnp.concatenate(diagonal + [tail, tail, empty], axis=0).T
        rows = jnp.where(odd_head == 1, turned[QBLK:], turned[:QBLK])
        out_ref[b * QBLK : (b + 1) * QBLK, :] = rows.astype(BF16)


def attend(phase, items, folded, arrays, state, wv_t):
    blocks = folded.shape[0]
    last = wv_t is not None
    sizes = [a.shape[0] for a in arrays]
    out_shape = [
        jax.ShapeDtypeStruct((blocks + 1, D, H * QBLK), F32),
        jax.ShapeDtypeStruct((blocks + 1, 8, H * QBLK), F32),
    ]
    args = [items, folded, *arrays]
    in_specs = [IN_SMEM, IN_VMEM] + [IN_VMEM] * len(arrays)
    scratch = [pltpu.VMEM((sum(sizes), D), BF16)] + [pltpu.VMEM((2 * SBLK, H * QBLK), F32)] * 2
    aliases = {}
    if phase:
        aliases = {len(args): 0, len(args) + 1: 1}
        args += list(state)
        in_specs += [IN_VMEM] * 2
    if last:
        args.append(wv_t)
        in_specs.append(IN_VMEM)
        out_shape.append(jax.ShapeDtypeStruct((blocks * QBLK, D + TAIL), BF16))
    return pl.pallas_call(
        functools.partial(attend_kernel, phase, sizes, last),
        out_shape=out_shape,
        in_specs=in_specs,
        out_specs=[IN_VMEM] * len(out_shape),
        input_output_aliases=aliases,
        scratch_shapes=scratch,
        compiler_params=pltpu.CompilerParams(vmem_limit_bytes=16 * MIB),
        cost_estimate=pl.CostEstimate(flops=1_000_000_000, bytes_accessed=4 * MIB, transcendentals=700_000),
        name="attend_%d" % phase,
    )(*args)


def finish_kernel(got_ref, queries, wo, gain, out_ref):
    sources, count, _ = got_ref.shape
    slot = lax.broadcasted_iota(jnp.int32, (TAIL, D), 0)
    pairs = H // 2
    head = 2 * lax.rem(slot, pairs) + lax.div(slot, 16)
    spread = (head == head_of_lane((TAIL, D))) & (lax.rem(slot, 16) < 3 * pairs) & (slot < 32)
    spread = jnp.where(spread, 1.0, 0.0).astype(BF16)
    tails = got_ref[:, :, D:].reshape(sources * count, TAIL)
    levels = jnp.dot(tails, spread, preferred_element_type=F32).reshape(sources, count, D)
    factors = jnp.exp2(levels - jnp.max(levels, axis=0, keepdims=True))
    mixed = jnp.sum(factors * got_ref[:, :, :D].astype(F32), axis=0)
    attended = (mixed / jnp.sum(factors, axis=0)).astype(BF16)
    rows = queries[...].astype(F32) + jnp.dot(attended, wo[...], preferred_element_type=F32)
    center = rows - jnp.mean(rows, axis=1, keepdims=True)
    variance = jnp.mean(center * center, axis=1, keepdims=True)
    updated = (center * lax.rsqrt(variance + 1e-05) * gain[...]).astype(BF16)
    for i in range(sources):
        out_ref[i] = updated


def finish(got, queries, w_out, norm_gain):
    sources, count, _ = got.shape
    return pl.pallas_call(
        finish_kernel,
        out_shape=jax.ShapeDtypeStruct((sources, count, D), BF16),
        in_specs=[IN_VMEM] * 4,
        out_specs=IN_VMEM,
        compiler_params=pltpu.CompilerParams(vmem_limit_bytes=16 * MIB),
        cost_estimate=pl.CostEstimate(flops=10_000_000, bytes_accessed=MIB, transcendentals=140_000),
        name="finish",
    )(got, queries, w_out, norm_gain)


STEP = 512
SLOTS = 4


def piece_row(place_ref, piece):
    ahead, other, row = piece
    index = place_ref[0]
    chip = lax.rem(lax.div(index, 2) + ahead + CHIPS, CHIPS)
    core = lax.rem(index, 2)
    core = 1 - core if other else core
    return (chip * 2 + core) * (OWN_BLOCKS * SBLK) + row


def logits_kernel(pieces, place_ref, updated_ref, wm, *rest):
    count = len(pieces)
    piece_refs = rest[:count]
    updated_out, out_ref, embed, tiles, in_sems, out_sems = rest[count:]
    keep = pltpu.make_async_copy(updated_ref, updated_out, in_sems.at[0])
    keep.start()
    rows = jnp.dot(updated_ref[...], wm[...], preferred_element_type=F32).astype(BF16)
    embed[...] = rows * (1.0 / math.sqrt(D))
    stores = []
    for i, ref in enumerate(piece_refs):
        for row in range(0, ref.shape[0], STEP):
            slot = len(stores) % SLOTS
            if len(stores) >= SLOTS:
                stores[-SLOTS].wait()
            tiles[slot] = lax.dot_general(
                embed[...], ref[row : row + STEP, :], NT, preferred_element_type=F32
            )
            column = pl.multiple_of(piece_row(place_ref, pieces[i]) + row, STEP)
            stores.append(
                pltpu.make_async_copy(tiles.at[slot], out_ref.at[:, pl.ds(column, STEP)], out_sems.at[slot])
            )
            stores[-1].start()
    for store in stores[-SLOTS:]:
        store.wait()
    keep.wait()


def logits(place, updated, w_mask, pieces, arrays):
    count = updated.shape[0]
    shard = sum(a.shape[0] for a in arrays)
    return pl.pallas_call(
        functools.partial(logits_kernel, pieces),
        out_shape=(
            jax.ShapeDtypeStruct(updated.shape, BF16),
            jax.ShapeDtypeStruct((count, shard), F32),
        ),
        in_specs=[IN_SMEM, IN_VMEM, IN_VMEM] + [IN_VMEM] * len(arrays),
        out_specs=(IN_HBM, IN_HBM),
        scratch_shapes=[
            pltpu.VMEM((count, D), BF16),
            pltpu.VMEM((SLOTS, count, STEP), F32),
            pltpu.SemaphoreType.DMA((1,)),
            pltpu.SemaphoreType.DMA((SLOTS,)),
        ],
        compiler_params=pltpu.CompilerParams(vmem_limit_bytes=16 * MIB),
        cost_estimate=pl.CostEstimate(
            flops=2 * count * shard * D, bytes_accessed=20 * MIB, transcendentals=0
        ),
        name="logits",
    )(place, updated, w_mask, *arrays)


def tied(first, second, state):
    first, state = lax.optimization_barrier((first, tuple(state)))
    second, state = lax.optimization_barrier((second, state))
    return first, second, state


def shards(queries, features, block_lists, w_query, w_key, w_value, w_out, norm_gain, w_mask):
    space = lax.axis_size("space")
    place = jnp.stack([lax.axis_index("query"), lax.axis_index("space")]).astype(jnp.int32)
    up = [(y * 2 + c, (y + 1) % CHIPS * 2 + c) for y in range(CHIPS) for c in range(2)]
    down = [(y * 2 + c, (y - 1) % CHIPS * 2 + c) for y in range(CHIPS) for c in range(2)]
    cores = [(i, i ^ 1) for i in range(2 * CHIPS)]

    def send(rows, pairs):
        return lax.ppermute(rows, "query", pairs)

    below = send(features, up)
    above = send(features, down)
    beside = send(features, cores)
    count = queries.shape[0] // space
    weights = (w_query, w_key, w_value, w_out, norm_gain, w_mask)
    folded, items, wv_t, w_out, norm_gain, w_mask, own, mine = project(
        place, count, block_lists.T, queries, *weights, features
    )
    state = attend(0, items, folded, [own, beside], None, None)
    half = features.shape[0] // 2
    below, above, state = tied(below, above, state)
    far_low = send(below[:half], up)
    far_high = send(above[half:], down)
    sent = lax.optimization_barrier((below, above))
    near = [below, send(sent[0], cores), above, send(sent[1], cores)]
    state = attend(1, items, folded, near, state, None)
    far_low, far_high, state = tied(far_low, far_high, state)
    far = [far_low, send(far_low, cores), far_high, send(far_high, cores)]
    partial = attend(2, items, folded, far, state, wv_t)[2]

    got = lax.all_to_all(partial.reshape(space, count, D + TAIL), "space", 0, 0)
    rows = finish(got, mine, w_out, norm_gain)
    updated = lax.all_to_all(rows, "space", 0, 0).reshape(queries.shape)
    pieces = [(0, False, 0), (0, True, 0), (-1, False, 0), (-1, True, 0), (1, False, 0), (1, True, 0)]
    pieces += [(-2, False, 0), (-2, True, 0), (2, False, half), (2, True, half)]
    return logits(place, updated, w_mask, pieces, [own, beside, *near, *far])


def solution(mesh):
    placed = (P("query", None), P(("space", "query"), None), P(), P(), P(), P(), P(), P(), P())
    return jax.shard_map(
        shards,
        mesh=mesh,
        in_specs=placed,
        out_specs=(P("query", None), P("query", "space")),
        check_vma=False,
    )
```

```python
import functools
import math

import jax
import jax.numpy as jnp
from jax import lax
from jax.experimental import pallas as pl
from jax.experimental.pallas import tpu as pltpu
from jax.sharding import PartitionSpec as P

D = 256
H = 8
HD = 32
QBLK = 64
SBLK = 128
CAP = 16
LOG2E = math.log2(math.e)
BF16 = jnp.bfloat16
F32 = jnp.float32
NT = (((1,), (1,)), ((), ()))
TN = (((0,), (0,)), ((), ()))
TAIL = 128
CHIPS = 4
OWN_BLOCKS = 8
SHARD_BLOCKS = 2 * CHIPS * OWN_BLOCKS
PHASES = 3
WIDTH = 20
LAST = 127
COUNTS = PHASES * WIDTH
PAIRS = H // 2
WIDE = 2 * QBLK
MIB = 1024 * 1024
IN_SMEM = pl.BlockSpec(memory_space=pltpu.SMEM)
IN_VMEM = pl.BlockSpec(memory_space=pltpu.VMEM)
IN_HBM = pl.BlockSpec(memory_space=pltpu.HBM)


def stay(array):
    return pltpu.with_memory_space_constraint(array, pltpu.HBM)


def head_of_lane(shape):
    return lax.broadcasted_iota(jnp.int32, shape, len(shape) - 1) // HD


def local_lists(place_ref, lists):
    chip, core = lax.div(place_ref[0], 2), lax.rem(place_ref[0], 2)
    inside = lax.rem(lists, OWN_BLOCKS)
    device = lax.rem(lax.div(lists, OWN_BLOCKS), 2 * CHIPS)
    other = jnp.where(lax.rem(device, 2) == core, 0, 1)
    ahead = lax.rem(lax.div(device, 2) - chip + CHIPS, CHIPS)
    toward = jnp.where(core == 0, CHIPS - 1, 1)
    near = (ahead == 1) | (ahead == CHIPS - 1)
    late = near & (ahead == toward) & (other == 1)
    position = jnp.where(near & (ahead != toward), 1 + other, jnp.where(near, 2 * other, other)) * OWN_BLOCKS + inside
    phase = jnp.where(ahead == 0, 0, jnp.where(near & ~late, 1, 2))
    phase = jnp.where(lax.div(lists, SHARD_BLOCKS) == place_ref[1], phase, -1)
    width = lists.shape[0]
    row = lax.broadcasted_iota(jnp.int32, (width, width), 0)
    column = lax.broadcasted_iota(jnp.int32, (width, width), 1)
    earlier = jnp.where(column < row, 1.0, 0.0).astype(BF16)
    code = jnp.full(lists.shape, -1.0, F32)
    for p in range(PHASES):
        mine = phase == p
        rank = jnp.dot(earlier, jnp.where(mine, 1.0, 0.0).astype(BF16), preferred_element_type=F32)
        code = jnp.where(mine, (p * WIDTH + rank) * 128.0 + position.astype(F32), code)
    return code


def write_items(ids, items, blocks):
    for phase in range(PHASES):

        def one_block(b, held):
            found = ids[b, COUNTS + phase]

            def one(i, held):
                first = ids[b, phase * WIDTH + 2 * i]
                alone = 2 * i + 1 >= found
                second = jnp.where(alone, first, ids[b, phase * WIDTH + 2 * i + 1])
                items[phase, held] = ((jnp.where(alone, 1, 0) * 64 + second) * 64 + first) * 16 + b
                return held + 1

            return lax.fori_loop(0, lax.div(found + 1, 2), one, held)

        total = lax.fori_loop(0, blocks, one_block, 0)
        items[phase, total] = blocks
        items[phase, total + 1] = blocks
        items[phase, LAST] = total


def project_kernel(place_ref, *refs):
    sources, rest = refs[:9], refs[9:]
    out_ref, items, wv_t, wo, gain, wm, own, mine, rest = *rest[:8], rest[8:]
    lists, queries, wq, wk, wv, ids, ids_smem, sems = rest
    blocks = out_ref.shape[0]
    count = mine.shape[0]
    lists_ref, queries_ref, wq_ref, wk_ref, wv_ref, wo_ref, gain_ref, wm_ref, own_ref = sources
    mine_ref = queries_ref.at[pl.ds(pl.multiple_of(place_ref[1] * count, count), count)]
    moves = [(lists_ref, lists), (queries_ref, queries), (wq_ref, wq), (wk_ref, wk), (wv_ref, wv)]
    moves += [(wo_ref, wo), (gain_ref, gain), (wm_ref, wm), (own_ref, own), (mine_ref, mine)]
    copies = [pltpu.make_async_copy(source, target, sems.at[i]) for i, (source, target) in enumerate(moves)]
    for copy in copies:
        copy.start()
    copies[0].wait()
    code = local_lists(place_ref, lists[...])
    list_row = lax.broadcasted_iota(jnp.int32, code.shape, 1)
    lane = lax.broadcasted_iota(jnp.int32, (code.shape[0], 128), 1)
    for b in range(blocks):
        wanted = place_ref[0] * blocks + b
        listed = jnp.sum(jnp.where(list_row == wanted, code, 0.0), axis=1, keepdims=True).astype(jnp.int32)
        slot = jnp.where(listed < 0, -1, lax.div(listed, 128))
        found = jnp.where(slot == lane, lax.rem(listed, 128), 0)
        phase = jnp.where(slot < 0, -1, lax.div(slot, WIDTH))
        found = found + jnp.where(phase == lane - COUNTS, jnp.where(phase < 0, 0, 1), 0)
        ids[b : b + 1, :] = jnp.sum(found.astype(F32), axis=0, keepdims=True).astype(jnp.int32)
    tell = pltpu.make_async_copy(ids, ids_smem, sems.at[len(moves)])
    tell.start()
    for copy in copies[1:]:
        copy.wait()
    wv_t[...] = wv[...].T
    proj = jnp.dot(queries[...], wq[...], preferred_element_type=F32).astype(BF16)
    head = head_of_lane((QBLK, D))
    scale = LOG2E / math.sqrt(HD)
    none = jnp.zeros((QBLK, D), BF16)
    for b in range(blocks):
        rows = proj[b * QBLK : (b + 1) * QBLK]
        for c in range(PAIRS):
            two = [jnp.where(head == h, rows, none) for h in (2 * c, 2 * c + 1)]
            folded = lax.dot_general(wk[...], jnp.concatenate(two, axis=0), NT, preferred_element_type=F32)
            out_ref[b, :, c * WIDE : (c + 1) * WIDE] = (folded * scale).astype(BF16)
    tell.wait()
    write_items(ids_smem, items, blocks)


def project(place, count, lists, queries, w_query, w_key, w_value, w_out, norm_gain, w_mask, features):
    blocks = queries.shape[0] // QBLK
    square = jax.ShapeDtypeStruct((D, D), BF16)
    gain = norm_gain.reshape(1, D)
    return pl.pallas_call(
        project_kernel,
        out_shape=(
            jax.ShapeDtypeStruct((blocks, D, H * QBLK), BF16),
            jax.ShapeDtypeStruct((8, 128), jnp.int32),
            square,
            square,
            jax.ShapeDtypeStruct(gain.shape, F32),
            square,
            jax.ShapeDtypeStruct(features.shape, BF16),
            jax.ShapeDtypeStruct((count, D), BF16),
        ),
        in_specs=[IN_SMEM] + [IN_HBM] * 9,
        out_specs=(IN_VMEM, IN_SMEM) + (IN_VMEM,) * 6,
        scratch_shapes=[
            pltpu.VMEM(lists.shape, jnp.int32),
            pltpu.VMEM(queries.shape, BF16),
            pltpu.VMEM((D, D), BF16),
            pltpu.VMEM((D, D), BF16),
            pltpu.VMEM((D, D), BF16),
            pltpu.VMEM((blocks, 128), jnp.int32),
            pltpu.SMEM((blocks, 128), jnp.int32),
            pltpu.SemaphoreType.DMA((11,)),
        ],
        compiler_params=pltpu.CompilerParams(vmem_limit_bytes=16 * MIB),
        cost_estimate=pl.CostEstimate(
            flops=2 * queries.shape[0] * D * D * (H + 1), bytes_accessed=3 * MIB, transcendentals=0
        ),
        name="project",
    )(place, *map(stay, (lists, queries, w_query, w_key, w_value, w_out, gain, w_mask, features)))


def keys_of(item, feats):
    rows = [lax.rem(lax.div(item, 16 * step), 64) * SBLK for step in (1, 64)]
    return jnp.concatenate([feats[pl.ds(pl.multiple_of(row, SBLK), SBLK), :] for row in rows], axis=0)


def score(item, feats, q_ref, scores):
    b = jnp.minimum(lax.rem(item, 16), q_ref.shape[0] - 1)
    scores[...] = jnp.dot(keys_of(item, feats), q_ref[b], preferred_element_type=F32)


def weigh(item, feats, scores, acc, stats):
    b = lax.rem(item, 16)
    turned = keys_of(item, feats).T
    alone = lax.div(item, 16 * 64 * 64) == 1
    halves = H * QBLK // 2
    for c in range(2):
        part = slice(c * halves, (c + 1) * halves)
        first = scores[:SBLK, part]
        second = jnp.where(alone, -jnp.inf, scores[SBLK:, part])
        top = stats[b, 0:1, part]
        higher = jnp.maximum(top, jnp.max(jnp.maximum(first, second), axis=0, keepdims=True))
        factor = jnp.exp2(top - higher)
        first = jnp.exp2(first - higher)
        second = jnp.exp2(second - higher)
        stats[b, 0:1, part] = higher
        stats[b, 1:2, part] = stats[b, 1:2, part] * factor + jnp.sum(first + second, axis=0, keepdims=True)
        weights = jnp.concatenate([first.astype(BF16), second.astype(BF16)], axis=0)
        acc[b, :, part] = acc[b, :, part] * factor + jnp.dot(turned, weights, preferred_element_type=F32)


def attend_kernel(phase, sizes, last, items, q_ref, *rest):
    count = len(sizes)
    piece_refs, rest = rest[:count], rest[count:]
    if phase:
        rest = rest[2:]
    if last:
        wv_t, acc, stats_ref, out_ref, feats, even, odd = rest
    else:
        acc, stats_ref, feats, even, odd = rest
    held = 0
    for size, ref in zip(sizes, piece_refs):
        feats[held : held + size, :] = ref[...]
        held += size
    if phase == 0:
        acc[...] = jnp.zeros(acc.shape, F32)
        stats_ref[:, 0:1, :] = jnp.full((acc.shape[0], 1, H * QBLK), -jnp.inf, F32)
        stats_ref[:, 1:2, :] = jnp.zeros((acc.shape[0], 1, H * QBLK), F32)
    score(items[phase, 0], feats, q_ref, even)

    def two_items(i, carry):
        score(items[phase, 2 * i + 1], feats, q_ref, odd)
        weigh(items[phase, 2 * i], feats, even, acc, stats_ref)
        score(items[phase, 2 * i + 2], feats, q_ref, even)
        weigh(items[phase, 2 * i + 1], feats, odd, acc, stats_ref)
        return carry

    lax.fori_loop(0, lax.div(items[phase, LAST] + 1, 2), two_items, 0)
    if not last:
        return
    slot = lax.broadcasted_iota(jnp.int32, (16, WIDE), 0)
    column = lax.broadcasted_iota(jnp.int32, (QBLK, D + TAIL), 1)
    odd_head = jnp.where(column < D, lax.rem(lax.div(column, HD), 2), lax.rem(lax.div(column, 16), 2))
    empty = jnp.zeros((TAIL - 32, WIDE), F32)
    for b in range(q_ref.shape[0]):
        diagonal = []
        tail = jnp.zeros((16, WIDE), F32)
        for c in range(PAIRS):
            part = slice(c * WIDE, (c + 1) * WIDE)
            total = stats_ref[b, 1:2, part]
            mean = (acc[b, :, part] * (1.0 / total)).astype(BF16)
            heads = slice(2 * HD * c, 2 * HD * (c + 1))
            diagonal.append(jnp.dot(wv_t[heads, :], mean, preferred_element_type=F32))
            level = stats_ref[b, 0:1, part] + jnp.log(total) * LOG2E
            for piece in range(3):
                rounded = level.astype(BF16).astype(F32)
                level = level - rounded
                tail = jnp.where(slot == piece * PAIRS + c, rounded, tail)
        turned = jnp.concatenate(diagonal + [tail, tail, empty], axis=0).T
        rows = jnp.where(odd_head == 1, turned[QBLK:], turned[:QBLK])
        out_ref[b * QBLK : (b + 1) * QBLK, :] = rows.astype(BF16)


def attend(phase, items, folded, arrays, state, wv_t):
    blocks = folded.shape[0]
    last = wv_t is not None
    sizes = [a.shape[0] for a in arrays]
    out_shape = [
        jax.ShapeDtypeStruct((blocks + 1, D, H * QBLK), F32),
        jax.ShapeDtypeStruct((blocks + 1, 8, H * QBLK), F32),
    ]
    args = [items, folded, *arrays]
    in_specs = [IN_SMEM, IN_VMEM] + [IN_VMEM] * len(arrays)
    scratch = [pltpu.VMEM((sum(sizes), D), BF16)] + [pltpu.VMEM((2 * SBLK, H * QBLK), F32)] * 2
    aliases = {}
    if phase:
        aliases = {len(args): 0, len(args) + 1: 1}
        args += list(state)
        in_specs += [IN_VMEM] * 2
    if last:
        args.append(wv_t)
        in_specs.append(IN_VMEM)
        out_shape.append(jax.ShapeDtypeStruct((blocks * QBLK, D + TAIL), BF16))
    return pl.pallas_call(
        functools.partial(attend_kernel, phase, sizes, last),
        out_shape=out_shape,
        in_specs=in_specs,
        out_specs=[IN_VMEM] * len(out_shape),
        input_output_aliases=aliases,
        scratch_shapes=scratch,
        compiler_params=pltpu.CompilerParams(vmem_limit_bytes=16 * MIB),
        cost_estimate=pl.CostEstimate(flops=1_000_000_000, bytes_accessed=4 * MIB, transcendentals=700_000),
        name="attend_%d" % phase,
    )(*args)


def finish_kernel(got_ref, queries, wo, gain, out_ref):
    sources, count, _ = got_ref.shape
    slot = lax.broadcasted_iota(jnp.int32, (TAIL, D), 0)
    pairs = H // 2
    head = 2 * lax.rem(slot, pairs) + lax.div(slot, 16)
    spread = (head == head_of_lane((TAIL, D))) & (lax.rem(slot, 16) < 3 * pairs) & (slot < 32)
    spread = jnp.where(spread, 1.0, 0.0).astype(BF16)
    tails = got_ref[:, :, D:].reshape(sources * count, TAIL)
    levels = jnp.dot(tails, spread, preferred_element_type=F32).reshape(sources, count, D)
    factors = jnp.exp2(levels - jnp.max(levels, axis=0, keepdims=True))
    mixed = jnp.sum(factors * got_ref[:, :, :D].astype(F32), axis=0)
    attended = (mixed / jnp.sum(factors, axis=0)).astype(BF16)
    rows = queries[...].astype(F32) + jnp.dot(attended, wo[...], preferred_element_type=F32)
    center = rows - jnp.mean(rows, axis=1, keepdims=True)
    variance = jnp.mean(center * center, axis=1, keepdims=True)
    updated = (center * lax.rsqrt(variance + 1e-05) * gain[...]).astype(BF16)
    for i in range(sources):
        out_ref[i] = updated


def finish(got, queries, w_out, norm_gain):
    sources, count, _ = got.shape
    return pl.pallas_call(
        finish_kernel,
        out_shape=jax.ShapeDtypeStruct((sources, count, D), BF16),
        in_specs=[IN_VMEM] * 4,
        out_specs=IN_VMEM,
        compiler_params=pltpu.CompilerParams(vmem_limit_bytes=16 * MIB),
        cost_estimate=pl.CostEstimate(flops=10_000_000, bytes_accessed=MIB, transcendentals=140_000),
        name="finish",
    )(got, queries, w_out, norm_gain)


STEP = 512
SLOTS = 4


def piece_row(place_ref, piece):
    ahead, other = piece
    chip, core = lax.div(place_ref[0], 2), lax.rem(place_ref[0], 2)
    chip = lax.rem(chip + jnp.where(core == 0, -ahead, ahead) + CHIPS, CHIPS)
    core = 1 - core if other else core
    return (chip * 2 + core) * (OWN_BLOCKS * SBLK)


def logits_kernel(pieces, place_ref, updated_ref, wm, *rest):
    count = len(pieces)
    piece_refs = rest[:count]
    updated_out, out_ref, embed, tiles, in_sems, out_sems = rest[count:]
    keep = pltpu.make_async_copy(updated_ref, updated_out, in_sems.at[0])
    keep.start()
    rows = jnp.dot(updated_ref[...], wm[...], preferred_element_type=F32).astype(BF16)
    embed[...] = rows * (1.0 / math.sqrt(D))
    stores = []
    for i, ref in enumerate(piece_refs):
        for row in range(0, ref.shape[0], STEP):
            slot = len(stores) % SLOTS
            if len(stores) >= SLOTS:
                stores[-SLOTS].wait()
            tiles[slot] = lax.dot_general(
                embed[...], ref[row : row + STEP, :], NT, preferred_element_type=F32
            )
            column = pl.multiple_of(piece_row(place_ref, pieces[i]) + row, STEP)
            stores.append(
                pltpu.make_async_copy(tiles.at[slot], out_ref.at[:, pl.ds(column, STEP)], out_sems.at[slot])
            )
            stores[-1].start()
    for store in stores[-SLOTS:]:
        store.wait()
    keep.wait()


def logits(place, updated, w_mask, pieces, arrays):
    count = updated.shape[0]
    shard = sum(a.shape[0] for a in arrays)
    return pl.pallas_call(
        functools.partial(logits_kernel, pieces),
        out_shape=(
            jax.ShapeDtypeStruct(updated.shape, BF16),
            jax.ShapeDtypeStruct((count, shard), F32),
        ),
        in_specs=[IN_SMEM, IN_VMEM, IN_VMEM] + [IN_VMEM] * len(arrays),
        out_specs=(IN_HBM, IN_HBM),
        scratch_shapes=[
            pltpu.VMEM((count, D), BF16),
            pltpu.VMEM((SLOTS, count, STEP), F32),
            pltpu.SemaphoreType.DMA((1,)),
            pltpu.SemaphoreType.DMA((SLOTS,)),
        ],
        compiler_params=pltpu.CompilerParams(vmem_limit_bytes=16 * MIB),
        cost_estimate=pl.CostEstimate(
            flops=2 * count * shard * D, bytes_accessed=20 * MIB, transcendentals=0
        ),
        name="logits",
    )(place, updated, w_mask, *arrays)


def shards(queries, features, block_lists, w_query, w_key, w_value, w_out, norm_gain, w_mask):
    space = lax.axis_size("space")
    place = jnp.stack([lax.axis_index("query"), lax.axis_index("space")]).astype(jnp.int32)
    ring = [(y * 2 + c, (y + 1 - 2 * c) % CHIPS * 2 + c) for y in range(CHIPS) for c in range(2)]
    back = [(to, source) for source, to in ring]
    cores = [(i, i ^ 1) for i in range(2 * CHIPS)]

    def send(rows, pairs):
        return lax.ppermute(rows, "query", pairs)

    came = send(features, ring)
    beside = send(features, cores)
    later, beside = lax.optimization_barrier((features, beside))
    back_came = send(later, back)
    count = queries.shape[0] // space
    weights = (w_query, w_key, w_value, w_out, norm_gain, w_mask)
    folded, items, wv_t, w_out, norm_gain, w_mask, own, mine = project(
        place, count, block_lists.T, queries, *weights, features
    )
    state = attend(0, items, folded, [own, beside], None, None)
    came, state = lax.optimization_barrier((came, tuple(state)))
    far = send(came, ring)
    near = [came, back_came, send(came, cores)]
    state = attend(1, items, folded, near, state, None)
    far, state = lax.optimization_barrier((far, tuple(state)))
    far = [far, send(far, cores), send(back_came, cores)]
    partial = attend(2, items, folded, far, state, wv_t)[2]

    got = lax.all_to_all(partial.reshape(space, count, D + TAIL), "space", 0, 0)
    rows = finish(got, mine, w_out, norm_gain)
    updated = lax.all_to_all(rows, "space", 0, 0).reshape(queries.shape)
    pieces = [(0, False), (0, True), (1, False), (-1, False), (-1, True), (2, False), (2, True), (1, True)]
    return logits(place, updated, w_mask, pieces, [own, beside, *near, *far])


def solution(mesh):
    placed = (P("query", None), P(("space", "query"), None), P(), P(), P(), P(), P(), P(), P())
    return jax.shard_map(
        shards,
        mesh=mesh,
        in_specs=placed,
        out_specs=(P("query", None), P("query", "space")),
        check_vma=False,
    )
```

```python
import functools
import math

import jax
import jax.numpy as jnp
from jax import lax
from jax.experimental import pallas as pl
from jax.experimental.pallas import tpu as pltpu
from jax.sharding import PartitionSpec as P

D = 256
H = 8
HD = 32
QBLK = 64
SBLK = 128
CAP = 16
LOG2E = math.log2(math.e)
BF16 = jnp.bfloat16
F32 = jnp.float32
NT = (((1,), (1,)), ((), ()))
TN = (((0,), (0,)), ((), ()))
TAIL = 128
CHIPS = 4
OWN_BLOCKS = 8
SHARD_BLOCKS = 2 * CHIPS * OWN_BLOCKS
PHASES = 3
WIDTH = 20
LAST = 127
COUNTS = PHASES * WIDTH
PAIRS = H // 2
WIDE = 2 * QBLK
MIB = 1024 * 1024
IN_SMEM = pl.BlockSpec(memory_space=pltpu.SMEM)
IN_VMEM = pl.BlockSpec(memory_space=pltpu.VMEM)
IN_HBM = pl.BlockSpec(memory_space=pltpu.HBM)


def stay(array):
    return pltpu.with_memory_space_constraint(array, pltpu.HBM)


def head_of_lane(shape):
    return lax.broadcasted_iota(jnp.int32, shape, len(shape) - 1) // HD


def local_lists(place_ref, lists):
    chip, core = lax.div(place_ref[0], 2), lax.rem(place_ref[0], 2)
    inside = lax.rem(lists, OWN_BLOCKS)
    device = lax.rem(lax.div(lists, OWN_BLOCKS), 2 * CHIPS)
    other = jnp.where(lax.rem(device, 2) == core, 0, 1)
    ahead = lax.rem(lax.div(device, 2) - chip + CHIPS, CHIPS)
    toward = jnp.where(core == 0, CHIPS - 1, 1)
    near = (ahead == 1) | (ahead == CHIPS - 1)
    late = near & (ahead == toward) & (other == 1)
    position = jnp.where(near & (ahead != toward), 1 + other, jnp.where(near, 2 * other, other)) * OWN_BLOCKS + inside
    phase = jnp.where(ahead == 0, 0, jnp.where(near & ~late, 1, 2))
    phase = jnp.where(lax.div(lists, SHARD_BLOCKS) == place_ref[1], phase, -1)
    width = lists.shape[0]
    row = lax.broadcasted_iota(jnp.int32, (width, width), 0)
    column = lax.broadcasted_iota(jnp.int32, (width, width), 1)
    earlier = jnp.where(column < row, 1.0, 0.0).astype(BF16)
    code = jnp.full(lists.shape, -1.0, F32)
    for p in range(PHASES):
        mine = phase == p
        rank = jnp.dot(earlier, jnp.where(mine, 1.0, 0.0).astype(BF16), preferred_element_type=F32)
        code = jnp.where(mine, (p * WIDTH + rank) * 128.0 + position.astype(F32), code)
    return code


def write_items(ids, items, blocks):
    for phase in range(PHASES):

        def one_block(b, held):
            found = ids[b, COUNTS + phase]

            def one(i, held):
                first = ids[b, phase * WIDTH + 2 * i]
                alone = 2 * i + 1 >= found
                second = jnp.where(alone, first, ids[b, phase * WIDTH + 2 * i + 1])
                items[phase, held] = ((jnp.where(alone, 1, 0) * 64 + second) * 64 + first) * 16 + b
                return held + 1

            return lax.fori_loop(0, lax.div(found + 1, 2), one, held)

        total = lax.fori_loop(0, blocks, one_block, 0)
        items[phase, total] = blocks
        items[phase, total + 1] = blocks
        items[phase, LAST] = total


def project_kernel(place_ref, *refs):
    sources, rest = refs[:9], refs[9:]
    out_ref, items, wv_t, wo, gain, wm, own, mine, rest = *rest[:8], rest[8:]
    lists, queries, wq, wk, wv, ids, ids_smem, sems = rest
    blocks = out_ref.shape[0]
    count = mine.shape[0]
    lists_ref, queries_ref, wq_ref, wk_ref, wv_ref, wo_ref, gain_ref, wm_ref, own_ref = sources
    mine_ref = queries_ref.at[pl.ds(pl.multiple_of(place_ref[1] * count, count), count)]
    moves = [(lists_ref, lists), (queries_ref, queries), (wq_ref, wq), (wk_ref, wk), (wv_ref, wv)]
    moves += [(wo_ref, wo), (gain_ref, gain), (wm_ref, wm), (own_ref, own), (mine_ref, mine)]
    copies = [pltpu.make_async_copy(source, target, sems.at[i]) for i, (source, target) in enumerate(moves)]
    for copy in copies:
        copy.start()
    copies[0].wait()
    code = local_lists(place_ref, lists[...])
    list_row = lax.broadcasted_iota(jnp.int32, code.shape, 1)
    lane = lax.broadcasted_iota(jnp.int32, (code.shape[0], 128), 1)
    for b in range(blocks):
        wanted = place_ref[0] * blocks + b
        listed = jnp.sum(jnp.where(list_row == wanted, code, 0.0), axis=1, keepdims=True).astype(jnp.int32)
        slot = jnp.where(listed < 0, -1, lax.div(listed, 128))
        found = jnp.where(slot == lane, lax.rem(listed, 128), 0)
        phase = jnp.where(slot < 0, -1, lax.div(slot, WIDTH))
        found = found + jnp.where(phase == lane - COUNTS, jnp.where(phase < 0, 0, 1), 0)
        ids[b : b + 1, :] = jnp.sum(found.astype(F32), axis=0, keepdims=True).astype(jnp.int32)
    tell = pltpu.make_async_copy(ids, ids_smem, sems.at[len(moves)])
    tell.start()
    for copy in copies[1:]:
        copy.wait()
    wv_t[...] = wv[...].T
    proj = jnp.dot(queries[...], wq[...], preferred_element_type=F32).astype(BF16)
    head = head_of_lane((QBLK, D))
    scale = LOG2E / math.sqrt(HD)
    none = jnp.zeros((QBLK, D), BF16)
    for b in range(blocks):
        rows = proj[b * QBLK : (b + 1) * QBLK]
        for c in range(PAIRS):
            two = [jnp.where(head == h, rows, none) for h in (2 * c, 2 * c + 1)]
            folded = lax.dot_general(wk[...], jnp.concatenate(two, axis=0), NT, preferred_element_type=F32)
            out_ref[b, :, c * WIDE : (c + 1) * WIDE] = (folded * scale).astype(BF16)
    tell.wait()
    write_items(ids_smem, items, blocks)


def project(place, count, lists, queries, w_query, w_key, w_value, w_out, norm_gain, w_mask, features):
    blocks = queries.shape[0] // QBLK
    square = jax.ShapeDtypeStruct((D, D), BF16)
    gain = norm_gain.reshape(1, D)
    return pl.pallas_call(
        project_kernel,
        out_shape=(
            jax.ShapeDtypeStruct((blocks, D, H * QBLK), BF16),
            jax.ShapeDtypeStruct((8, 128), jnp.int32),
            square,
            square,
            jax.ShapeDtypeStruct(gain.shape, F32),
            square,
            jax.ShapeDtypeStruct(features.shape, BF16),
            jax.ShapeDtypeStruct((count, D), BF16),
        ),
        in_specs=[IN_SMEM] + [IN_HBM] * 9,
        out_specs=(IN_VMEM, IN_SMEM) + (IN_VMEM,) * 6,
        scratch_shapes=[
            pltpu.VMEM(lists.shape, jnp.int32),
            pltpu.VMEM(queries.shape, BF16),
            pltpu.VMEM((D, D), BF16),
            pltpu.VMEM((D, D), BF16),
            pltpu.VMEM((D, D), BF16),
            pltpu.VMEM((blocks, 128), jnp.int32),
            pltpu.SMEM((blocks, 128), jnp.int32),
            pltpu.SemaphoreType.DMA((11,)),
        ],
        compiler_params=pltpu.CompilerParams(vmem_limit_bytes=16 * MIB),
        cost_estimate=pl.CostEstimate(
            flops=2 * queries.shape[0] * D * D * (H + 1), bytes_accessed=3 * MIB, transcendentals=0
        ),
        name="project",
    )(place, *map(stay, (lists, queries, w_query, w_key, w_value, w_out, gain, w_mask, features)))


def keys_of(item, feats):
    rows = [lax.rem(lax.div(item, 16 * step), 64) * SBLK for step in (1, 64)]
    return jnp.concatenate([feats[pl.ds(pl.multiple_of(row, SBLK), SBLK), :] for row in rows], axis=0)


def score(item, feats, q_ref, scores):
    b = jnp.minimum(lax.rem(item, 16), q_ref.shape[0] - 1)
    scores[...] = jnp.dot(keys_of(item, feats), q_ref[b], preferred_element_type=F32)


def weigh(item, feats, scores, acc, stats):
    b = lax.rem(item, 16)
    turned = keys_of(item, feats).T
    alone = lax.div(item, 16 * 64 * 64) == 1
    halves = H * QBLK // 2
    for c in range(2):
        part = slice(c * halves, (c + 1) * halves)
        first = scores[:SBLK, part]
        second = jnp.where(alone, -jnp.inf, scores[SBLK:, part])
        top = stats[b, 0:1, part]
        higher = jnp.maximum(top, jnp.max(jnp.maximum(first, second), axis=0, keepdims=True))
        factor = jnp.exp2(top - higher)
        first = jnp.exp2(first - higher)
        second = jnp.exp2(second - higher)
        stats[b, 0:1, part] = higher
        stats[b, 1:2, part] = stats[b, 1:2, part] * factor + jnp.sum(first + second, axis=0, keepdims=True)
        weights = jnp.concatenate([first.astype(BF16), second.astype(BF16)], axis=0)
        acc[b, :, part] = acc[b, :, part] * factor + jnp.dot(turned, weights, preferred_element_type=F32)


def attend_kernel(phase, sizes, last, items, q_ref, *rest):
    count = len(sizes)
    piece_refs, rest = rest[:count], rest[count:]
    if phase:
        rest = rest[2:]
    if last:
        wv_t, acc, stats_ref, out_ref, feats, even, odd = rest
    else:
        acc, stats_ref, feats, even, odd = rest
    held = 0
    for size, ref in zip(sizes, piece_refs):
        feats[held : held + size, :] = ref[...]
        held += size
    if phase == 0:
        acc[...] = jnp.zeros(acc.shape, F32)
        stats_ref[:, 0:1, :] = jnp.full((acc.shape[0], 1, H * QBLK), -jnp.inf, F32)
        stats_ref[:, 1:2, :] = jnp.zeros((acc.shape[0], 1, H * QBLK), F32)
    score(items[phase, 0], feats, q_ref, even)

    def two_items(i, carry):
        score(items[phase, 2 * i + 1], feats, q_ref, odd)
        weigh(items[phase, 2 * i], feats, even, acc, stats_ref)
        score(items[phase, 2 * i + 2], feats, q_ref, even)
        weigh(items[phase, 2 * i + 1], feats, odd, acc, stats_ref)
        return carry

    lax.fori_loop(0, lax.div(items[phase, LAST] + 1, 2), two_items, 0)
    if not last:
        return
    slot = lax.broadcasted_iota(jnp.int32, (16, WIDE), 0)
    column = lax.broadcasted_iota(jnp.int32, (QBLK, D + TAIL), 1)
    odd_head = jnp.where(column < D, lax.rem(lax.div(column, HD), 2), lax.rem(lax.div(column, 16), 2))
    empty = jnp.zeros((TAIL - 32, WIDE), F32)
    for b in range(q_ref.shape[0]):
        diagonal = []
        tail = jnp.zeros((16, WIDE), F32)
        for c in range(PAIRS):
            part = slice(c * WIDE, (c + 1) * WIDE)
            total = stats_ref[b, 1:2, part]
            mean = (acc[b, :, part] * (1.0 / total)).astype(BF16)
            heads = slice(2 * HD * c, 2 * HD * (c + 1))
            diagonal.append(jnp.dot(wv_t[heads, :], mean, preferred_element_type=F32))
            level = stats_ref[b, 0:1, part] + jnp.log(total) * LOG2E
            for piece in range(3):
                rounded = level.astype(BF16).astype(F32)
                level = level - rounded
                tail = jnp.where(slot == piece * PAIRS + c, rounded, tail)
        turned = jnp.concatenate(diagonal + [tail, tail, empty], axis=0).T
        rows = jnp.where(odd_head == 1, turned[QBLK:], turned[:QBLK])
        out_ref[b * QBLK : (b + 1) * QBLK, :] = rows.astype(BF16)


def attend(phase, items, folded, arrays, state, wv_t):
    blocks = folded.shape[0]
    last = wv_t is not None
    sizes = [a.shape[0] for a in arrays]
    out_shape = [
        jax.ShapeDtypeStruct((blocks + 1, D, H * QBLK), F32),
        jax.ShapeDtypeStruct((blocks + 1, 8, H * QBLK), F32),
    ]
    args = [items, folded, *arrays]
    in_specs = [IN_SMEM, IN_VMEM] + [IN_VMEM] * len(arrays)
    scratch = [pltpu.VMEM((sum(sizes), D), BF16)] + [pltpu.VMEM((2 * SBLK, H * QBLK), F32)] * 2
    aliases = {}
    if phase:
        aliases = {len(args): 0, len(args) + 1: 1}
        args += list(state)
        in_specs += [IN_VMEM] * 2
    if last:
        args.append(wv_t)
        in_specs.append(IN_VMEM)
        out_shape.append(jax.ShapeDtypeStruct((blocks * QBLK, D + TAIL), BF16))
    return pl.pallas_call(
        functools.partial(attend_kernel, phase, sizes, last),
        out_shape=out_shape,
        in_specs=in_specs,
        out_specs=[IN_VMEM] * len(out_shape),
        input_output_aliases=aliases,
        scratch_shapes=scratch,
        compiler_params=pltpu.CompilerParams(vmem_limit_bytes=16 * MIB),
        cost_estimate=pl.CostEstimate(flops=1_000_000_000, bytes_accessed=4 * MIB, transcendentals=700_000),
        name="attend_%d" % phase,
    )(*args)


def finish_kernel(got_ref, queries, wo, gain, out_ref):
    sources, count, _ = got_ref.shape
    slot = lax.broadcasted_iota(jnp.int32, (TAIL, D), 0)
    pairs = H // 2
    head = 2 * lax.rem(slot, pairs) + lax.div(slot, 16)
    spread = (head == head_of_lane((TAIL, D))) & (lax.rem(slot, 16) < 3 * pairs) & (slot < 32)
    spread = jnp.where(spread, 1.0, 0.0).astype(BF16)
    tails = got_ref[:, :, D:].reshape(sources * count, TAIL)
    levels = jnp.dot(tails, spread, preferred_element_type=F32).reshape(sources, count, D)
    factors = jnp.exp2(levels - jnp.max(levels, axis=0, keepdims=True))
    mixed = jnp.sum(factors * got_ref[:, :, :D].astype(F32), axis=0)
    attended = (mixed / jnp.sum(factors, axis=0)).astype(BF16)
    rows = queries[...].astype(F32) + jnp.dot(attended, wo[...], preferred_element_type=F32)
    center = rows - jnp.mean(rows, axis=1, keepdims=True)
    variance = jnp.mean(center * center, axis=1, keepdims=True)
    updated = (center * lax.rsqrt(variance + 1e-05) * gain[...]).astype(BF16)
    for i in range(sources):
        out_ref[i] = updated


def finish(got, queries, w_out, norm_gain):
    sources, count, _ = got.shape
    return pl.pallas_call(
        finish_kernel,
        out_shape=jax.ShapeDtypeStruct((sources, count, D), BF16),
        in_specs=[IN_VMEM] * 4,
        out_specs=IN_VMEM,
        compiler_params=pltpu.CompilerParams(vmem_limit_bytes=16 * MIB),
        cost_estimate=pl.CostEstimate(flops=10_000_000, bytes_accessed=MIB, transcendentals=140_000),
        name="finish",
    )(got, queries, w_out, norm_gain)


STEP = 512
SLOTS = 4


def piece_row(place_ref, piece):
    ahead, other = piece
    chip, core = lax.div(place_ref[0], 2), lax.rem(place_ref[0], 2)
    chip = lax.rem(chip + jnp.where(core == 0, -ahead, ahead) + CHIPS, CHIPS)
    core = 1 - core if other else core
    return (chip * 2 + core) * (OWN_BLOCKS * SBLK)


def logits_kernel(pieces, place_ref, updated_ref, wm, *rest):
    count = len(pieces)
    piece_refs = rest[:count]
    updated_out, out_ref, embed, tiles, in_sems, out_sems = rest[count:]
    keep = pltpu.make_async_copy(updated_ref, updated_out, in_sems.at[0])
    keep.start()
    rows = jnp.dot(updated_ref[...], wm[...], preferred_element_type=F32).astype(BF16)
    embed[...] = rows * (1.0 / math.sqrt(D))
    stores = []
    for i, ref in enumerate(piece_refs):
        for row in range(0, ref.shape[0], STEP):
            slot = len(stores) % SLOTS
            if len(stores) >= SLOTS:
                stores[-SLOTS].wait()
            tiles[slot] = lax.dot_general(
                embed[...], ref[row : row + STEP, :], NT, preferred_element_type=F32
            )
            column = pl.multiple_of(piece_row(place_ref, pieces[i]) + row, STEP)
            stores.append(
                pltpu.make_async_copy(tiles.at[slot], out_ref.at[:, pl.ds(column, STEP)], out_sems.at[slot])
            )
            stores[-1].start()
    for store in stores[-SLOTS:]:
        store.wait()
    keep.wait()


def logits(place, updated, w_mask, pieces, arrays):
    count = updated.shape[0]
    shard = sum(a.shape[0] for a in arrays)
    return pl.pallas_call(
        functools.partial(logits_kernel, pieces),
        out_shape=(
            jax.ShapeDtypeStruct(updated.shape, BF16),
            jax.ShapeDtypeStruct((count, shard), F32),
        ),
        in_specs=[IN_SMEM, IN_VMEM, IN_VMEM] + [IN_VMEM] * len(arrays),
        out_specs=(IN_HBM, IN_HBM),
        scratch_shapes=[
            pltpu.VMEM((count, D), BF16),
            pltpu.VMEM((SLOTS, count, STEP), F32),
            pltpu.SemaphoreType.DMA((1,)),
            pltpu.SemaphoreType.DMA((SLOTS,)),
        ],
        compiler_params=pltpu.CompilerParams(vmem_limit_bytes=16 * MIB),
        cost_estimate=pl.CostEstimate(
            flops=2 * count * shard * D, bytes_accessed=20 * MIB, transcendentals=0
        ),
        name="logits",
    )(place, updated, w_mask, *arrays)


def shards(queries, features, block_lists, w_query, w_key, w_value, w_out, norm_gain, w_mask):
    space = lax.axis_size("space")
    place = jnp.stack([lax.axis_index("query"), lax.axis_index("space")]).astype(jnp.int32)
    ring = [(y * 2 + c, (y + 1 - 2 * c) % CHIPS * 2 + c) for y in range(CHIPS) for c in range(2)]
    back = [(to, source) for source, to in ring]
    cores = [(i, i ^ 1) for i in range(2 * CHIPS)]

    def send(rows, pairs):
        return lax.ppermute(rows, "query", pairs)

    came = send(features, ring)
    beside = send(features, cores)
    count = queries.shape[0] // space
    weights = (w_query, w_key, w_value, w_out, norm_gain, w_mask)
    folded, items, wv_t, w_out, norm_gain, w_mask, own, mine = project(
        place, count, block_lists.T, queries, *weights, features
    )
    later, folded = lax.optimization_barrier((features, folded))
    back_came = send(later, back)
    state = attend(0, items, folded, [own, beside], None, None)
    came, state = lax.optimization_barrier((came, tuple(state)))
    far = send(came, ring)
    near = [came, back_came, send(came, cores)]
    state = attend(1, items, folded, near, state, None)
    far, state = lax.optimization_barrier((far, tuple(state)))
    far = [far, send(far, cores), send(back_came, cores)]
    partial = attend(2, items, folded, far, state, wv_t)[2]

    got = lax.all_to_all(partial.reshape(space, count, D + TAIL), "space", 0, 0)
    rows = finish(got, mine, w_out, norm_gain)
    updated = lax.all_to_all(rows, "space", 0, 0).reshape(queries.shape)
    pieces = [(0, False), (0, True), (1, False), (-1, False), (-1, True), (2, False), (2, True), (1, True)]
    return logits(place, updated, w_mask, pieces, [own, beside, *near, *far])


def solution(mesh):
    placed = (P("query", None), P(("space", "query"), None), P(), P(), P(), P(), P(), P(), P())
    return jax.shard_map(
        shards,
        mesh=mesh,
        in_specs=placed,
        out_specs=(P("query", None), P("query", "space")),
        check_vma=False,
    )
```

```python
import functools
import math

import jax
import jax.numpy as jnp
from jax import lax
from jax.experimental import pallas as pl
from jax.experimental.pallas import tpu as pltpu
from jax.sharding import PartitionSpec as P

D = 256
H = 8
HD = 32
QBLK = 64
SBLK = 128
CAP = 16
LOG2E = math.log2(math.e)
BF16 = jnp.bfloat16
F32 = jnp.float32
NT = (((1,), (1,)), ((), ()))
TN = (((0,), (0,)), ((), ()))
TAIL = 128
CHIPS = 4
OWN_BLOCKS = 8
SHARD_BLOCKS = 2 * CHIPS * OWN_BLOCKS
PHASES = 3
WIDTH = 20
LAST = 127
COUNTS = PHASES * WIDTH
PAIRS = H // 2
WIDE = 2 * QBLK
MIB = 1024 * 1024
IN_SMEM = pl.BlockSpec(memory_space=pltpu.SMEM)
IN_VMEM = pl.BlockSpec(memory_space=pltpu.VMEM)
IN_HBM = pl.BlockSpec(memory_space=pltpu.HBM)


def stay(array):
    return pltpu.with_memory_space_constraint(array, pltpu.HBM)


def head_of_lane(shape):
    return lax.broadcasted_iota(jnp.int32, shape, len(shape) - 1) // HD


def local_lists(place_ref, lists):
    chip, core = lax.div(place_ref[0], 2), lax.rem(place_ref[0], 2)
    inside = lax.rem(lists, OWN_BLOCKS)
    device = lax.rem(lax.div(lists, OWN_BLOCKS), 2 * CHIPS)
    other = jnp.where(lax.rem(device, 2) == core, 0, 1)
    ahead = lax.rem(lax.div(device, 2) - chip + CHIPS, CHIPS)
    toward = jnp.where(core == 0, CHIPS - 1, 1)
    near = (ahead == 1) | (ahead == CHIPS - 1)
    late = near & (ahead == toward) & (other == 1)
    position = jnp.where(near & (ahead != toward), 1 + other, jnp.where(near, 2 * other, other)) * OWN_BLOCKS + inside
    phase = jnp.where(ahead == 0, 0, jnp.where(near & ~late, 1, 2))
    phase = jnp.where(lax.div(lists, SHARD_BLOCKS) == place_ref[1], phase, -1)
    width = lists.shape[0]
    row = lax.broadcasted_iota(jnp.int32, (width, width), 0)
    column = lax.broadcasted_iota(jnp.int32, (width, width), 1)
    earlier = jnp.where(column < row, 1.0, 0.0).astype(BF16)
    code = jnp.full(lists.shape, -1.0, F32)
    for p in range(PHASES):
        mine = phase == p
        rank = jnp.dot(earlier, jnp.where(mine, 1.0, 0.0).astype(BF16), preferred_element_type=F32)
        code = jnp.where(mine, (p * WIDTH + rank) * 128.0 + position.astype(F32), code)
    return code


def write_items(ids, items, blocks):
    for phase in range(PHASES):

        def one_block(b, held):
            found = ids[b, COUNTS + phase]

            def one(i, held):
                first = ids[b, phase * WIDTH + 2 * i]
                alone = 2 * i + 1 >= found
                second = jnp.where(alone, first, ids[b, phase * WIDTH + 2 * i + 1])
                items[phase, held] = ((jnp.where(alone, 1, 0) * 64 + second) * 64 + first) * 16 + b
                return held + 1

            return lax.fori_loop(0, lax.div(found + 1, 2), one, held)

        total = lax.fori_loop(0, blocks, one_block, 0)
        items[phase, total] = blocks
        items[phase, total + 1] = blocks
        items[phase, LAST] = total


def project_kernel(place_ref, *refs):
    sources, rest = refs[:9], refs[9:]
    out_ref, items, wv_t, wo, gain, wm, own, mine, rest = *rest[:8], rest[8:]
    lists, queries, wq, wk, wv, ids, ids_smem, sems = rest
    blocks = out_ref.shape[0]
    count = mine.shape[0]
    lists_ref, queries_ref, wq_ref, wk_ref, wv_ref, wo_ref, gain_ref, wm_ref, own_ref = sources
    mine_ref = queries_ref.at[pl.ds(pl.multiple_of(place_ref[1] * count, count), count)]
    moves = [(lists_ref, lists), (queries_ref, queries), (wq_ref, wq), (wk_ref, wk), (wv_ref, wv)]
    moves += [(wo_ref, wo), (gain_ref, gain), (wm_ref, wm), (own_ref, own), (mine_ref, mine)]
    copies = [pltpu.make_async_copy(source, target, sems.at[i]) for i, (source, target) in enumerate(moves)]
    for copy in copies:
        copy.start()
    copies[0].wait()
    code = local_lists(place_ref, lists[...])
    list_row = lax.broadcasted_iota(jnp.int32, code.shape, 1)
    lane = lax.broadcasted_iota(jnp.int32, (code.shape[0], 128), 1)
    for b in range(blocks):
        wanted = place_ref[0] * blocks + b
        listed = jnp.sum(jnp.where(list_row == wanted, code, 0.0), axis=1, keepdims=True).astype(jnp.int32)
        slot = jnp.where(listed < 0, -1, lax.div(listed, 128))
        found = jnp.where(slot == lane, lax.rem(listed, 128), 0)
        phase = jnp.where(slot < 0, -1, lax.div(slot, WIDTH))
        found = found + jnp.where(phase == lane - COUNTS, jnp.where(phase < 0, 0, 1), 0)
        ids[b : b + 1, :] = jnp.sum(found.astype(F32), axis=0, keepdims=True).astype(jnp.int32)
    tell = pltpu.make_async_copy(ids, ids_smem, sems.at[len(moves)])
    tell.start()
    for copy in copies[1:]:
        copy.wait()
    wv_t[...] = wv[...].T
    proj = jnp.dot(queries[...], wq[...], preferred_element_type=F32).astype(BF16)
    head = head_of_lane((QBLK, D))
    scale = LOG2E / math.sqrt(HD)
    none = jnp.zeros((QBLK, D), BF16)
    for b in range(blocks):
        rows = proj[b * QBLK : (b + 1) * QBLK]
        for c in range(PAIRS):
            two = [jnp.where(head == h, rows, none) for h in (2 * c, 2 * c + 1)]
            folded = lax.dot_general(wk[...], jnp.concatenate(two, axis=0), NT, preferred_element_type=F32)
            out_ref[b, :, c * WIDE : (c + 1) * WIDE] = (folded * scale).astype(BF16)
    tell.wait()
    write_items(ids_smem, items, blocks)


def project(place, count, lists, queries, w_query, w_key, w_value, w_out, norm_gain, w_mask, features):
    blocks = queries.shape[0] // QBLK
    square = jax.ShapeDtypeStruct((D, D), BF16)
    gain = norm_gain.reshape(1, D)
    return pl.pallas_call(
        project_kernel,
        out_shape=(
            jax.ShapeDtypeStruct((blocks, D, H * QBLK), BF16),
            jax.ShapeDtypeStruct((8, 128), jnp.int32),
            square,
            square,
            jax.ShapeDtypeStruct(gain.shape, F32),
            square,
            jax.ShapeDtypeStruct(features.shape, BF16),
            jax.ShapeDtypeStruct((count, D), BF16),
        ),
        in_specs=[IN_SMEM] + [IN_HBM] * 9,
        out_specs=(IN_VMEM, IN_SMEM) + (IN_VMEM,) * 6,
        scratch_shapes=[
            pltpu.VMEM(lists.shape, jnp.int32),
            pltpu.VMEM(queries.shape, BF16),
            pltpu.VMEM((D, D), BF16),
            pltpu.VMEM((D, D), BF16),
            pltpu.VMEM((D, D), BF16),
            pltpu.VMEM((blocks, 128), jnp.int32),
            pltpu.SMEM((blocks, 128), jnp.int32),
            pltpu.SemaphoreType.DMA((11,)),
        ],
        compiler_params=pltpu.CompilerParams(vmem_limit_bytes=16 * MIB),
        cost_estimate=pl.CostEstimate(
            flops=2 * queries.shape[0] * D * D * (H + 1), bytes_accessed=3 * MIB, transcendentals=0
        ),
        name="project",
    )(place, *map(stay, (lists, queries, w_query, w_key, w_value, w_out, gain, w_mask, features)))


def keys_of(item, feats):
    rows = [lax.rem(lax.div(item, 16 * step), 64) * SBLK for step in (1, 64)]
    return jnp.concatenate([feats[pl.ds(pl.multiple_of(row, SBLK), SBLK), :] for row in rows], axis=0)


def score(item, feats, q_ref, scores):
    b = jnp.minimum(lax.rem(item, 16), q_ref.shape[0] - 1)
    scores[...] = jnp.dot(keys_of(item, feats), q_ref[b], preferred_element_type=F32)


def weigh(item, feats, scores, acc, stats):
    b = lax.rem(item, 16)
    turned = keys_of(item, feats).T
    alone = lax.div(item, 16 * 64 * 64) == 1
    halves = H * QBLK // 2
    for c in range(2):
        part = slice(c * halves, (c + 1) * halves)
        first = scores[:SBLK, part]
        second = jnp.where(alone, -jnp.inf, scores[SBLK:, part])
        top = stats[b, 0:1, part]
        higher = jnp.maximum(top, jnp.max(jnp.maximum(first, second), axis=0, keepdims=True))
        factor = jnp.exp2(top - higher)
        first = jnp.exp2(first - higher)
        second = jnp.exp2(second - higher)
        stats[b, 0:1, part] = higher
        stats[b, 1:2, part] = stats[b, 1:2, part] * factor + jnp.sum(first + second, axis=0, keepdims=True)
        weights = jnp.concatenate([first.astype(BF16), second.astype(BF16)], axis=0)
        acc[b, :, part] = acc[b, :, part] * factor + jnp.dot(turned, weights, preferred_element_type=F32)


def attend_kernel(phase, sizes, last, items, q_ref, *rest):
    count = len(sizes)
    piece_refs, rest = rest[:count], rest[count:]
    if phase:
        rest = rest[2:]
    if last:
        wv_t, acc, stats_ref, out_ref, feats, even, odd = rest
    else:
        acc, stats_ref, feats, even, odd = rest
    held = 0
    for size, ref in zip(sizes, piece_refs):
        feats[held : held + size, :] = ref[...]
        held += size
    if phase == 0:
        acc[...] = jnp.zeros(acc.shape, F32)
        stats_ref[:, 0:1, :] = jnp.full((acc.shape[0], 1, H * QBLK), -jnp.inf, F32)
        stats_ref[:, 1:2, :] = jnp.zeros((acc.shape[0], 1, H * QBLK), F32)
    score(items[phase, 0], feats, q_ref, even)

    def two_items(i, carry):
        score(items[phase, 2 * i + 1], feats, q_ref, odd)
        weigh(items[phase, 2 * i], feats, even, acc, stats_ref)
        score(items[phase, 2 * i + 2], feats, q_ref, even)
        weigh(items[phase, 2 * i + 1], feats, odd, acc, stats_ref)
        return carry

    lax.fori_loop(0, lax.div(items[phase, LAST] + 1, 2), two_items, 0)
    if not last:
        return
    slot = lax.broadcasted_iota(jnp.int32, (16, WIDE), 0)
    column = lax.broadcasted_iota(jnp.int32, (QBLK, D + TAIL), 1)
    odd_head = jnp.where(column < D, lax.rem(lax.div(column, HD), 2), lax.rem(lax.div(column, 16), 2))
    empty = jnp.zeros((TAIL - 32, WIDE), F32)
    for b in range(q_ref.shape[0]):
        diagonal = []
        tail = jnp.zeros((16, WIDE), F32)
        for two in range(PAIRS // 2):
            part = slice(two * 2 * WIDE, (two + 1) * 2 * WIDE)
            total = stats_ref[b, 1:2, part]
            mean = (acc[b, :, part] * (1.0 / total)).astype(BF16)
            heads = slice(4 * HD * two, 4 * HD * (two + 1))
            values = jnp.dot(wv_t[heads, :], mean, preferred_element_type=F32)
            diagonal += [values[: 2 * HD, :WIDE], values[2 * HD :, WIDE:]]
            level = stats_ref[b, 0:1, part] + jnp.log(total) * LOG2E
            for piece in range(3):
                rounded = level.astype(BF16).astype(F32)
                level = level - rounded
                for k in range(2):
                    at = piece * PAIRS + 2 * two + k
                    tail = jnp.where(slot == at, rounded[:, k * WIDE : (k + 1) * WIDE], tail)
        turned = jnp.concatenate(diagonal + [tail, tail, empty], axis=0).T
        rows = jnp.where(odd_head == 1, turned[QBLK:], turned[:QBLK])
        out_ref[b * QBLK : (b + 1) * QBLK, :] = rows.astype(BF16)


def attend(phase, items, folded, arrays, state, wv_t):
    blocks = folded.shape[0]
    last = wv_t is not None
    sizes = [a.shape[0] for a in arrays]
    out_shape = [
        jax.ShapeDtypeStruct((blocks + 1, D, H * QBLK), F32),
        jax.ShapeDtypeStruct((blocks + 1, 8, H * QBLK), F32),
    ]
    args = [items, folded, *arrays]
    in_specs = [IN_SMEM, IN_VMEM] + [IN_VMEM] * len(arrays)
    scratch = [pltpu.VMEM((sum(sizes), D), BF16)] + [pltpu.VMEM((2 * SBLK, H * QBLK), F32)] * 2
    aliases = {}
    if phase:
        aliases = {len(args): 0, len(args) + 1: 1}
        args += list(state)
        in_specs += [IN_VMEM] * 2
    if last:
        args.append(wv_t)
        in_specs.append(IN_VMEM)
        out_shape.append(jax.ShapeDtypeStruct((blocks * QBLK, D + TAIL), BF16))
    return pl.pallas_call(
        functools.partial(attend_kernel, phase, sizes, last),
        out_shape=out_shape,
        in_specs=in_specs,
        out_specs=[IN_VMEM] * len(out_shape),
        input_output_aliases=aliases,
        scratch_shapes=scratch,
        compiler_params=pltpu.CompilerParams(vmem_limit_bytes=16 * MIB),
        cost_estimate=pl.CostEstimate(flops=1_000_000_000, bytes_accessed=4 * MIB, transcendentals=700_000),
        name="attend_%d" % phase,
    )(*args)


def finish_kernel(got_ref, queries, wo, gain, out_ref):
    sources, count, _ = got_ref.shape
    slot = lax.broadcasted_iota(jnp.int32, (TAIL, D), 0)
    pairs = H // 2
    head = 2 * lax.rem(slot, pairs) + lax.div(slot, 16)
    spread = (head == head_of_lane((TAIL, D))) & (lax.rem(slot, 16) < 3 * pairs) & (slot < 32)
    spread = jnp.where(spread, 1.0, 0.0).astype(BF16)
    tails = got_ref[:, :, D:].reshape(sources * count, TAIL)
    levels = jnp.dot(tails, spread, preferred_element_type=F32).reshape(sources, count, D)
    factors = jnp.exp2(levels - jnp.max(levels, axis=0, keepdims=True))
    mixed = jnp.sum(factors * got_ref[:, :, :D].astype(F32), axis=0)
    attended = (mixed / jnp.sum(factors, axis=0)).astype(BF16)
    rows = queries[...].astype(F32) + jnp.dot(attended, wo[...], preferred_element_type=F32)
    center = rows - jnp.mean(rows, axis=1, keepdims=True)
    variance = jnp.mean(center * center, axis=1, keepdims=True)
    updated = (center * lax.rsqrt(variance + 1e-05) * gain[...]).astype(BF16)
    for i in range(sources):
        out_ref[i] = updated


def finish(got, queries, w_out, norm_gain):
    sources, count, _ = got.shape
    return pl.pallas_call(
        finish_kernel,
        out_shape=jax.ShapeDtypeStruct((sources, count, D), BF16),
        in_specs=[IN_VMEM] * 4,
        out_specs=IN_VMEM,
        compiler_params=pltpu.CompilerParams(vmem_limit_bytes=16 * MIB),
        cost_estimate=pl.CostEstimate(flops=10_000_000, bytes_accessed=MIB, transcendentals=140_000),
        name="finish",
    )(got, queries, w_out, norm_gain)


STEP = 512
SLOTS = 4


def piece_row(place_ref, piece):
    ahead, other = piece
    chip, core = lax.div(place_ref[0], 2), lax.rem(place_ref[0], 2)
    chip = lax.rem(chip + jnp.where(core == 0, -ahead, ahead) + CHIPS, CHIPS)
    core = 1 - core if other else core
    return (chip * 2 + core) * (OWN_BLOCKS * SBLK)


def logits_kernel(pieces, place_ref, updated_ref, wm, *rest):
    count = len(pieces)
    piece_refs = rest[:count]
    updated_out, out_ref, embed, tiles, in_sems, out_sems = rest[count:]
    keep = pltpu.make_async_copy(updated_ref, updated_out, in_sems.at[0])
    keep.start()
    rows = jnp.dot(updated_ref[...], wm[...], preferred_element_type=F32).astype(BF16)
    embed[...] = rows * (1.0 / math.sqrt(D))
    stores = []
    for i, ref in enumerate(piece_refs):
        for row in range(0, ref.shape[0], STEP):
            slot = len(stores) % SLOTS
            if len(stores) >= SLOTS:
                stores[-SLOTS].wait()
            tiles[slot] = lax.dot_general(
                embed[...], ref[row : row + STEP, :], NT, preferred_element_type=F32
            )
            column = pl.multiple_of(piece_row(place_ref, pieces[i]) + row, STEP)
            stores.append(
                pltpu.make_async_copy(tiles.at[slot], out_ref.at[:, pl.ds(column, STEP)], out_sems.at[slot])
            )
            stores[-1].start()
    for store in stores[-SLOTS:]:
        store.wait()
    keep.wait()


def logits(place, updated, w_mask, pieces, arrays):
    count = updated.shape[0]
    shard = sum(a.shape[0] for a in arrays)
    return pl.pallas_call(
        functools.partial(logits_kernel, pieces),
        out_shape=(
            jax.ShapeDtypeStruct(updated.shape, BF16),
            jax.ShapeDtypeStruct((count, shard), F32),
        ),
        in_specs=[IN_SMEM, IN_VMEM, IN_VMEM] + [IN_VMEM] * len(arrays),
        out_specs=(IN_HBM, IN_HBM),
        scratch_shapes=[
            pltpu.VMEM((count, D), BF16),
            pltpu.VMEM((SLOTS, count, STEP), F32),
            pltpu.SemaphoreType.DMA((1,)),
            pltpu.SemaphoreType.DMA((SLOTS,)),
        ],
        compiler_params=pltpu.CompilerParams(vmem_limit_bytes=16 * MIB),
        cost_estimate=pl.CostEstimate(
            flops=2 * count * shard * D, bytes_accessed=20 * MIB, transcendentals=0
        ),
        name="logits",
    )(place, updated, w_mask, *arrays)


def shards(queries, features, block_lists, w_query, w_key, w_value, w_out, norm_gain, w_mask):
    space = lax.axis_size("space")
    place = jnp.stack([lax.axis_index("query"), lax.axis_index("space")]).astype(jnp.int32)
    ring = [(y * 2 + c, (y + 1 - 2 * c) % CHIPS * 2 + c) for y in range(CHIPS) for c in range(2)]
    back = [(to, source) for source, to in ring]
    cores = [(i, i ^ 1) for i in range(2 * CHIPS)]

    def send(rows, pairs):
        return lax.ppermute(rows, "query", pairs)

    came = send(features, ring)
    beside = send(features, cores)
    count = queries.shape[0] // space
    weights = (w_query, w_key, w_value, w_out, norm_gain, w_mask)
    folded, items, wv_t, w_out, norm_gain, w_mask, own, mine = project(
        place, count, block_lists.T, queries, *weights, features
    )
    later, folded = lax.optimization_barrier((features, folded))
    back_came = send(later, back)
    state = attend(0, items, folded, [own, beside], None, None)
    came, state = lax.optimization_barrier((came, tuple(state)))
    far = send(came, ring)
    near = [came, back_came, send(came, cores)]
    state = attend(1, items, folded, near, state, None)
    far, state = lax.optimization_barrier((far, tuple(state)))
    far = [far, send(far, cores), send(back_came, cores)]
    partial = attend(2, items, folded, far, state, wv_t)[2]

    got = lax.all_to_all(partial.reshape(space, count, D + TAIL), "space", 0, 0)
    rows = finish(got, mine, w_out, norm_gain)
    updated = lax.all_to_all(rows, "space", 0, 0).reshape(queries.shape)
    pieces = [(0, False), (0, True), (1, False), (-1, False), (-1, True), (2, False), (2, True), (1, True)]
    return logits(place, updated, w_mask, pieces, [own, beside, *near, *far])


def solution(mesh):
    placed = (P("query", None), P(("space", "query"), None), P(), P(), P(), P(), P(), P(), P())
    return jax.shard_map(
        shards,
        mesh=mesh,
        in_specs=placed,
        out_specs=(P("query", None), P("query", "space")),
        check_vma=False,
    )
```

```python
import functools
import math

import jax
import jax.numpy as jnp
from jax import lax
from jax.experimental import pallas as pl
from jax.experimental.pallas import tpu as pltpu
from jax.sharding import PartitionSpec as P

D = 256
H = 8
HD = 32
QBLK = 64
SBLK = 128
CAP = 16
LOG2E = math.log2(math.e)
BF16 = jnp.bfloat16
F32 = jnp.float32
NT = (((1,), (1,)), ((), ()))
TN = (((0,), (0,)), ((), ()))
TAIL = 128
CHIPS = 4
OWN_BLOCKS = 8
SHARD_BLOCKS = 2 * CHIPS * OWN_BLOCKS
PHASES = 4
WIDTH = 20
LAST = 127
COUNTS = PHASES * WIDTH
PAIRS = H // 2
WIDE = 2 * QBLK
MIB = 1024 * 1024
IN_SMEM = pl.BlockSpec(memory_space=pltpu.SMEM)
IN_VMEM = pl.BlockSpec(memory_space=pltpu.VMEM)
IN_HBM = pl.BlockSpec(memory_space=pltpu.HBM)


def stay(array):
    return pltpu.with_memory_space_constraint(array, pltpu.HBM)


def head_of_lane(shape):
    return lax.broadcasted_iota(jnp.int32, shape, len(shape) - 1) // HD


def local_lists(place_ref, lists):
    chip, core = lax.div(place_ref[0], 2), lax.rem(place_ref[0], 2)
    inside = lax.rem(lists, OWN_BLOCKS)
    device = lax.rem(lax.div(lists, OWN_BLOCKS), 2 * CHIPS)
    other = jnp.where(lax.rem(device, 2) == core, 0, 1)
    ahead = lax.rem(lax.div(device, 2) - chip + CHIPS, CHIPS)
    toward = jnp.where(core == 0, CHIPS - 1, 1)
    near = (ahead == 1) | (ahead == CHIPS - 1)
    late = near & (ahead == toward) & (other == 1)
    away = jnp.where(near & (ahead != toward), 1 + other, 0)
    position = jnp.where(late, 1, away) * OWN_BLOCKS + inside
    position = jnp.where(ahead == 0, other * OWN_BLOCKS + inside, position)
    phase = jnp.where(ahead == 0, 0, jnp.where(near & ~late, 1, jnp.where(late | (other == 0), 2, 3)))
    phase = jnp.where(lax.div(lists, SHARD_BLOCKS) == place_ref[1], phase, -1)
    width = lists.shape[0]
    row = lax.broadcasted_iota(jnp.int32, (width, width), 0)
    column = lax.broadcasted_iota(jnp.int32, (width, width), 1)
    earlier = jnp.where(column < row, 1.0, 0.0).astype(BF16)
    code = jnp.full(lists.shape, -1.0, F32)
    for p in range(PHASES):
        mine = phase == p
        rank = jnp.dot(earlier, jnp.where(mine, 1.0, 0.0).astype(BF16), preferred_element_type=F32)
        code = jnp.where(mine, (p * WIDTH + rank) * 128.0 + position.astype(F32), code)
    return code


def write_items(ids, items, blocks):
    for phase in range(PHASES):

        def one_block(b, held):
            found = ids[b, COUNTS + phase]

            def one(i, held):
                first = ids[b, phase * WIDTH + 2 * i]
                alone = 2 * i + 1 >= found
                second = jnp.where(alone, first, ids[b, phase * WIDTH + 2 * i + 1])
                items[phase, held] = ((jnp.where(alone, 1, 0) * 64 + second) * 64 + first) * 16 + b
                return held + 1

            return lax.fori_loop(0, lax.div(found + 1, 2), one, held)

        total = lax.fori_loop(0, blocks, one_block, 0)
        items[phase, total] = blocks
        items[phase, total + 1] = blocks
        items[phase, LAST] = total


def project_kernel(place_ref, *refs):
    sources, rest = refs[:9], refs[9:]
    out_ref, items, wv_t, wo, gain, wm, own, mine, rest = *rest[:8], rest[8:]
    lists, queries, wq, wk, wv, ids, ids_smem, sems = rest
    blocks = out_ref.shape[0]
    count = mine.shape[0]
    lists_ref, queries_ref, wq_ref, wk_ref, wv_ref, wo_ref, gain_ref, wm_ref, own_ref = sources
    mine_ref = queries_ref.at[pl.ds(pl.multiple_of(place_ref[1] * count, count), count)]
    moves = [(lists_ref, lists), (queries_ref, queries), (wq_ref, wq), (wk_ref, wk), (wv_ref, wv)]
    moves += [(wo_ref, wo), (gain_ref, gain), (wm_ref, wm), (own_ref, own), (mine_ref, mine)]
    copies = [pltpu.make_async_copy(source, target, sems.at[i]) for i, (source, target) in enumerate(moves)]
    for copy in copies:
        copy.start()
    copies[0].wait()
    code = local_lists(place_ref, lists[...])
    list_row = lax.broadcasted_iota(jnp.int32, code.shape, 1)
    lane = lax.broadcasted_iota(jnp.int32, (code.shape[0], 128), 1)
    for b in range(blocks):
        wanted = place_ref[0] * blocks + b
        listed = jnp.sum(jnp.where(list_row == wanted, code, 0.0), axis=1, keepdims=True).astype(jnp.int32)
        slot = jnp.where(listed < 0, -1, lax.div(listed, 128))
        found = jnp.where(slot == lane, lax.rem(listed, 128), 0)
        phase = jnp.where(slot < 0, -1, lax.div(slot, WIDTH))
        found = found + jnp.where(phase == lane - COUNTS, jnp.where(phase < 0, 0, 1), 0)
        ids[b : b + 1, :] = jnp.sum(found.astype(F32), axis=0, keepdims=True).astype(jnp.int32)
    tell = pltpu.make_async_copy(ids, ids_smem, sems.at[len(moves)])
    tell.start()
    for copy in copies[1:]:
        copy.wait()
    wv_t[...] = wv[...].T
    proj = jnp.dot(queries[...], wq[...], preferred_element_type=F32).astype(BF16)
    head = head_of_lane((QBLK, D))
    scale = LOG2E / math.sqrt(HD)
    none = jnp.zeros((QBLK, D), BF16)
    for b in range(blocks):
        rows = proj[b * QBLK : (b + 1) * QBLK]
        for c in range(PAIRS):
            two = [jnp.where(head == h, rows, none) for h in (2 * c, 2 * c + 1)]
            folded = lax.dot_general(wk[...], jnp.concatenate(two, axis=0), NT, preferred_element_type=F32)
            out_ref[b, :, c * WIDE : (c + 1) * WIDE] = (folded * scale).astype(BF16)
    tell.wait()
    write_items(ids_smem, items, blocks)


def project(place, count, lists, queries, w_query, w_key, w_value, w_out, norm_gain, w_mask, features):
    blocks = queries.shape[0] // QBLK
    square = jax.ShapeDtypeStruct((D, D), BF16)
    gain = norm_gain.reshape(1, D)
    return pl.pallas_call(
        project_kernel,
        out_shape=(
            jax.ShapeDtypeStruct((blocks, D, H * QBLK), BF16),
            jax.ShapeDtypeStruct((8, 128), jnp.int32),
            square,
            square,
            jax.ShapeDtypeStruct(gain.shape, F32),
            square,
            jax.ShapeDtypeStruct(features.shape, BF16),
            jax.ShapeDtypeStruct((count, D), BF16),
        ),
        in_specs=[IN_SMEM] + [IN_HBM] * 9,
        out_specs=(IN_VMEM, IN_SMEM) + (IN_VMEM,) * 6,
        scratch_shapes=[
            pltpu.VMEM(lists.shape, jnp.int32),
            pltpu.VMEM(queries.shape, BF16),
            pltpu.VMEM((D, D), BF16),
            pltpu.VMEM((D, D), BF16),
            pltpu.VMEM((D, D), BF16),
            pltpu.VMEM((blocks, 128), jnp.int32),
            pltpu.SMEM((blocks, 128), jnp.int32),
            pltpu.SemaphoreType.DMA((11,)),
        ],
        compiler_params=pltpu.CompilerParams(vmem_limit_bytes=16 * MIB),
        cost_estimate=pl.CostEstimate(
            flops=2 * queries.shape[0] * D * D * (H + 1), bytes_accessed=3 * MIB, transcendentals=0
        ),
        name="project",
    )(place, *map(stay, (lists, queries, w_query, w_key, w_value, w_out, gain, w_mask, features)))


def keys_of(item, feats):
    rows = [lax.rem(lax.div(item, 16 * step), 64) * SBLK for step in (1, 64)]
    return jnp.concatenate([feats[pl.ds(pl.multiple_of(row, SBLK), SBLK), :] for row in rows], axis=0)


def score(item, feats, q_ref, scores):
    b = jnp.minimum(lax.rem(item, 16), q_ref.shape[0] - 1)
    scores[...] = jnp.dot(keys_of(item, feats), q_ref[b], preferred_element_type=F32)


def weigh(item, feats, scores, acc, stats):
    b = lax.rem(item, 16)
    turned = keys_of(item, feats).T
    alone = lax.div(item, 16 * 64 * 64) == 1
    halves = H * QBLK // 2
    for c in range(2):
        part = slice(c * halves, (c + 1) * halves)
        first = scores[:SBLK, part]
        second = jnp.where(alone, -jnp.inf, scores[SBLK:, part])
        top = stats[b, 0:1, part]
        higher = jnp.maximum(top, jnp.max(jnp.maximum(first, second), axis=0, keepdims=True))
        factor = jnp.exp2(top - higher)
        first = jnp.exp2(first - higher)
        second = jnp.exp2(second - higher)
        stats[b, 0:1, part] = higher
        stats[b, 1:2, part] = stats[b, 1:2, part] * factor + jnp.sum(first + second, axis=0, keepdims=True)
        weights = jnp.concatenate([first.astype(BF16), second.astype(BF16)], axis=0)
        acc[b, :, part] = acc[b, :, part] * factor + jnp.dot(turned, weights, preferred_element_type=F32)


def attend_kernel(phase, sizes, last, items, q_ref, *rest):
    count = len(sizes)
    piece_refs, rest = rest[:count], rest[count:]
    if phase:
        rest = rest[2:]
    if last:
        wv_t, acc, stats_ref, out_ref, feats, even, odd = rest
    else:
        acc, stats_ref, feats, even, odd = rest
    held = 0
    for size, ref in zip(sizes, piece_refs):
        feats[held : held + size, :] = ref[...]
        held += size
    if phase == 0:
        acc[...] = jnp.zeros(acc.shape, F32)
        stats_ref[:, 0:1, :] = jnp.full((acc.shape[0], 1, H * QBLK), -jnp.inf, F32)
        stats_ref[:, 1:2, :] = jnp.zeros((acc.shape[0], 1, H * QBLK), F32)
    score(items[phase, 0], feats, q_ref, even)

    def two_items(i, carry):
        score(items[phase, 2 * i + 1], feats, q_ref, odd)
        weigh(items[phase, 2 * i], feats, even, acc, stats_ref)
        score(items[phase, 2 * i + 2], feats, q_ref, even)
        weigh(items[phase, 2 * i + 1], feats, odd, acc, stats_ref)
        return carry

    lax.fori_loop(0, lax.div(items[phase, LAST] + 1, 2), two_items, 0)
    if not last:
        return
    slot = lax.broadcasted_iota(jnp.int32, (16, WIDE), 0)
    column = lax.broadcasted_iota(jnp.int32, (QBLK, D + TAIL), 1)
    odd_head = jnp.where(column < D, lax.rem(lax.div(column, HD), 2), lax.rem(lax.div(column, 16), 2))
    empty = jnp.zeros((TAIL - 32, WIDE), F32)
    for b in range(q_ref.shape[0]):
        diagonal = []
        tail = jnp.zeros((16, WIDE), F32)
        for two in range(PAIRS // 2):
            part = slice(two * 2 * WIDE, (two + 1) * 2 * WIDE)
            total = stats_ref[b, 1:2, part]
            mean = (acc[b, :, part] * (1.0 / total)).astype(BF16)
            heads = slice(4 * HD * two, 4 * HD * (two + 1))
            values = jnp.dot(wv_t[heads, :], mean, preferred_element_type=F32)
            diagonal += [values[: 2 * HD, :WIDE], values[2 * HD :, WIDE:]]
            level = stats_ref[b, 0:1, part] + jnp.log(total) * LOG2E
            for piece in range(3):
                rounded = level.astype(BF16).astype(F32)
                level = level - rounded
                for k in range(2):
                    at = piece * PAIRS + 2 * two + k
                    tail = jnp.where(slot == at, rounded[:, k * WIDE : (k + 1) * WIDE], tail)
        turned = jnp.concatenate(diagonal + [tail, tail, empty], axis=0).T
        rows = jnp.where(odd_head == 1, turned[QBLK:], turned[:QBLK])
        out_ref[b * QBLK : (b + 1) * QBLK, :] = rows.astype(BF16)


def attend(phase, items, folded, arrays, state, wv_t):
    blocks = folded.shape[0]
    last = wv_t is not None
    sizes = [a.shape[0] for a in arrays]
    out_shape = [
        jax.ShapeDtypeStruct((blocks + 1, D, H * QBLK), F32),
        jax.ShapeDtypeStruct((blocks + 1, 8, H * QBLK), F32),
    ]
    args = [items, folded, *arrays]
    in_specs = [IN_SMEM, IN_VMEM] + [IN_VMEM] * len(arrays)
    scratch = [pltpu.VMEM((sum(sizes), D), BF16)] + [pltpu.VMEM((2 * SBLK, H * QBLK), F32)] * 2
    aliases = {}
    if phase:
        aliases = {len(args): 0, len(args) + 1: 1}
        args += list(state)
        in_specs += [IN_VMEM] * 2
    if last:
        args.append(wv_t)
        in_specs.append(IN_VMEM)
        out_shape.append(jax.ShapeDtypeStruct((blocks * QBLK, D + TAIL), BF16))
    return pl.pallas_call(
        functools.partial(attend_kernel, phase, sizes, last),
        out_shape=out_shape,
        in_specs=in_specs,
        out_specs=[IN_VMEM] * len(out_shape),
        input_output_aliases=aliases,
        scratch_shapes=scratch,
        compiler_params=pltpu.CompilerParams(vmem_limit_bytes=16 * MIB),
        cost_estimate=pl.CostEstimate(flops=1_000_000_000, bytes_accessed=4 * MIB, transcendentals=700_000),
        name="attend_%d" % phase,
    )(*args)


def finish_kernel(got_ref, queries, wo, gain, out_ref):
    sources, count, _ = got_ref.shape
    slot = lax.broadcasted_iota(jnp.int32, (TAIL, D), 0)
    pairs = H // 2
    head = 2 * lax.rem(slot, pairs) + lax.div(slot, 16)
    spread = (head == head_of_lane((TAIL, D))) & (lax.rem(slot, 16) < 3 * pairs) & (slot < 32)
    spread = jnp.where(spread, 1.0, 0.0).astype(BF16)
    tails = got_ref[:, :, D:].reshape(sources * count, TAIL)
    levels = jnp.dot(tails, spread, preferred_element_type=F32).reshape(sources, count, D)
    factors = jnp.exp2(levels - jnp.max(levels, axis=0, keepdims=True))
    mixed = jnp.sum(factors * got_ref[:, :, :D].astype(F32), axis=0)
    attended = (mixed / jnp.sum(factors, axis=0)).astype(BF16)
    rows = queries[...].astype(F32) + jnp.dot(attended, wo[...], preferred_element_type=F32)
    center = rows - jnp.mean(rows, axis=1, keepdims=True)
    variance = jnp.mean(center * center, axis=1, keepdims=True)
    updated = (center * lax.rsqrt(variance + 1e-05) * gain[...]).astype(BF16)
    for i in range(sources):
        out_ref[i] = updated


def finish(got, queries, w_out, norm_gain):
    sources, count, _ = got.shape
    return pl.pallas_call(
        finish_kernel,
        out_shape=jax.ShapeDtypeStruct((sources, count, D), BF16),
        in_specs=[IN_VMEM] * 4,
        out_specs=IN_VMEM,
        compiler_params=pltpu.CompilerParams(vmem_limit_bytes=16 * MIB),
        cost_estimate=pl.CostEstimate(flops=10_000_000, bytes_accessed=MIB, transcendentals=140_000),
        name="finish",
    )(got, queries, w_out, norm_gain)


STEP = 512
SLOTS = 4


def piece_row(place_ref, piece):
    ahead, other = piece
    chip, core = lax.div(place_ref[0], 2), lax.rem(place_ref[0], 2)
    chip = lax.rem(chip + jnp.where(core == 0, -ahead, ahead) + CHIPS, CHIPS)
    core = 1 - core if other else core
    return (chip * 2 + core) * (OWN_BLOCKS * SBLK)


def logits_kernel(pieces, place_ref, updated_ref, wm, *rest):
    count = len(pieces)
    piece_refs = rest[:count]
    updated_out, out_ref, embed, tiles, in_sems, out_sems = rest[count:]
    keep = pltpu.make_async_copy(updated_ref, updated_out, in_sems.at[0])
    keep.start()
    rows = jnp.dot(updated_ref[...], wm[...], preferred_element_type=F32).astype(BF16)
    embed[...] = rows * (1.0 / math.sqrt(D))
    stores = []
    for i, ref in enumerate(piece_refs):
        for row in range(0, ref.shape[0], STEP):
            slot = len(stores) % SLOTS
            if len(stores) >= SLOTS:
                stores[-SLOTS].wait()
            tiles[slot] = lax.dot_general(
                embed[...], ref[row : row + STEP, :], NT, preferred_element_type=F32
            )
            column = pl.multiple_of(piece_row(place_ref, pieces[i]) + row, STEP)
            stores.append(
                pltpu.make_async_copy(tiles.at[slot], out_ref.at[:, pl.ds(column, STEP)], out_sems.at[slot])
            )
            stores[-1].start()
    for store in stores[-SLOTS:]:
        store.wait()
    keep.wait()


def logits(place, updated, w_mask, pieces, arrays):
    count = updated.shape[0]
    shard = sum(a.shape[0] for a in arrays)
    return pl.pallas_call(
        functools.partial(logits_kernel, pieces),
        out_shape=(
            jax.ShapeDtypeStruct(updated.shape, BF16),
            jax.ShapeDtypeStruct((count, shard), F32),
        ),
        in_specs=[IN_SMEM, IN_VMEM, IN_VMEM] + [IN_VMEM] * len(arrays),
        out_specs=(IN_HBM, IN_HBM),
        scratch_shapes=[
            pltpu.VMEM((count, D), BF16),
            pltpu.VMEM((SLOTS, count, STEP), F32),
            pltpu.SemaphoreType.DMA((1,)),
            pltpu.SemaphoreType.DMA((SLOTS,)),
        ],
        compiler_params=pltpu.CompilerParams(vmem_limit_bytes=16 * MIB),
        cost_estimate=pl.CostEstimate(
            flops=2 * count * shard * D, bytes_accessed=20 * MIB, transcendentals=0
        ),
        name="logits",
    )(place, updated, w_mask, *arrays)


def shards(queries, features, block_lists, w_query, w_key, w_value, w_out, norm_gain, w_mask):
    space = lax.axis_size("space")
    place = jnp.stack([lax.axis_index("query"), lax.axis_index("space")]).astype(jnp.int32)
    ring = [(y * 2 + c, (y + 1 - 2 * c) % CHIPS * 2 + c) for y in range(CHIPS) for c in range(2)]
    back = [(to, source) for source, to in ring]
    cores = [(i, i ^ 1) for i in range(2 * CHIPS)]

    def send(rows, pairs):
        return lax.ppermute(rows, "query", pairs)

    came = send(features, ring)
    beside = send(features, cores)
    count = queries.shape[0] // space
    weights = (w_query, w_key, w_value, w_out, norm_gain, w_mask)
    folded, items, wv_t, w_out, norm_gain, w_mask, own, mine = project(
        place, count, block_lists.T, queries, *weights, features
    )
    later, folded = lax.optimization_barrier((features, folded))
    back_came = send(later, back)
    state = attend(0, items, folded, [own, beside], None, None)
    came, state = lax.optimization_barrier((came, tuple(state)))
    far = send(came, ring)
    near = [came, back_came, send(came, cores)]
    state = attend(1, items, folded, near, state, None)
    far, state = lax.optimization_barrier((far, tuple(state)))
    final = [far, send(back_came, cores), send(far, cores)]
    state = attend(2, items, folded, final[:2], state, None)
    partial = attend(3, items, folded, final[2:], state, wv_t)[2]

    got = lax.all_to_all(partial.reshape(space, count, D + TAIL), "space", 0, 0)
    rows = finish(got, mine, w_out, norm_gain)
    updated = lax.all_to_all(rows, "space", 0, 0).reshape(queries.shape)
    pieces = [(0, False), (0, True), (1, False), (-1, False), (-1, True), (2, False), (1, True), (2, True)]
    return logits(place, updated, w_mask, pieces, [own, beside, *near, *final])


def solution(mesh):
    placed = (P("query", None), P(("space", "query"), None), P(), P(), P(), P(), P(), P(), P())
    return jax.shard_map(
        shards,
        mesh=mesh,
        in_specs=placed,
        out_specs=(P("query", None), P("query", "space")),
        check_vma=False,
    )
```

```python
import functools
import math

import jax
import jax.numpy as jnp
from jax import lax
from jax.experimental import pallas as pl
from jax.experimental.pallas import tpu as pltpu
from jax.sharding import PartitionSpec as P

D = 256
H = 8
HD = 32
QBLK = 64
SBLK = 128
CAP = 16
LOG2E = math.log2(math.e)
BF16 = jnp.bfloat16
F32 = jnp.float32
NT = (((1,), (1,)), ((), ()))
TN = (((0,), (0,)), ((), ()))
TAIL = 128
CHIPS = 4
OWN_BLOCKS = 8
SHARD_BLOCKS = 2 * CHIPS * OWN_BLOCKS
PHASES = 4
WIDTH = 20
LAST = 127
COUNTS = PHASES * WIDTH
PAIRS = H // 2
WIDE = 2 * QBLK
MIB = 1024 * 1024
IN_SMEM = pl.BlockSpec(memory_space=pltpu.SMEM)
IN_VMEM = pl.BlockSpec(memory_space=pltpu.VMEM)
IN_HBM = pl.BlockSpec(memory_space=pltpu.HBM)


def stay(array):
    return pltpu.with_memory_space_constraint(array, pltpu.HBM)


def head_of_lane(shape):
    return lax.broadcasted_iota(jnp.int32, shape, len(shape) - 1) // HD


def local_lists(place_ref, lists):
    chip, core = lax.div(place_ref[0], 2), lax.rem(place_ref[0], 2)
    inside = lax.rem(lists, OWN_BLOCKS)
    device = lax.rem(lax.div(lists, OWN_BLOCKS), 2 * CHIPS)
    other = jnp.where(lax.rem(device, 2) == core, 0, 1)
    ahead = lax.rem(lax.div(device, 2) - chip + CHIPS, CHIPS)
    toward = jnp.where(core == 0, CHIPS - 1, 1)
    near = (ahead == 1) | (ahead == CHIPS - 1)
    late = near & (ahead == toward) & (other == 1)
    away = jnp.where(near & (ahead != toward), 1 + other, 0)
    position = jnp.where(late, 1, away) * OWN_BLOCKS + inside
    position = jnp.where(ahead == 0, other * OWN_BLOCKS + inside, position)
    phase = jnp.where(ahead == 0, 0, jnp.where(near & ~late, 1, jnp.where(late | (other == 0), 2, 3)))
    phase = jnp.where(lax.div(lists, SHARD_BLOCKS) == place_ref[1], phase, -1)
    width = lists.shape[0]
    row = lax.broadcasted_iota(jnp.int32, (width, width), 0)
    column = lax.broadcasted_iota(jnp.int32, (width, width), 1)
    earlier = jnp.where(column < row, 1.0, 0.0).astype(BF16)
    code = jnp.full(lists.shape, -1.0, F32)
    for p in range(PHASES):
        mine = phase == p
        rank = jnp.dot(earlier, jnp.where(mine, 1.0, 0.0).astype(BF16), preferred_element_type=F32)
        code = jnp.where(mine, (p * WIDTH + rank) * 128.0 + position.astype(F32), code)
    return code


def write_items(ids, items, blocks):
    for phase in range(PHASES):

        def one_block(b, held):
            found = ids[b, COUNTS + phase]

            def one(i, held):
                first = ids[b, phase * WIDTH + 2 * i]
                alone = 2 * i + 1 >= found
                second = jnp.where(alone, first, ids[b, phase * WIDTH + 2 * i + 1])
                items[phase, held] = ((jnp.where(alone, 1, 0) * 64 + second) * 64 + first) * 16 + b
                return held + 1

            return lax.fori_loop(0, lax.div(found + 1, 2), one, held)

        total = lax.fori_loop(0, blocks, one_block, 0)
        items[phase, total] = blocks
        items[phase, total + 1] = blocks
        items[phase, LAST] = total


def project_kernel(place_ref, *refs):
    sources, rest = refs[:9], refs[9:]
    out_ref, items, wv_t, wo, gain, wm, own, mine, rest = *rest[:8], rest[8:]
    lists, queries, wq, wk, wv, ids, ids_smem, sems = rest
    blocks = out_ref.shape[0]
    count = mine.shape[0]
    lists_ref, queries_ref, wq_ref, wk_ref, wv_ref, wo_ref, gain_ref, wm_ref, own_ref = sources
    mine_ref = queries_ref.at[pl.ds(pl.multiple_of(place_ref[1] * count, count), count)]
    moves = [(lists_ref, lists), (queries_ref, queries), (wq_ref, wq), (wk_ref, wk), (wv_ref, wv)]
    moves += [(wo_ref, wo), (gain_ref, gain), (wm_ref, wm), (own_ref, own), (mine_ref, mine)]
    copies = [pltpu.make_async_copy(source, target, sems.at[i]) for i, (source, target) in enumerate(moves)]
    for copy in copies:
        copy.start()
    copies[0].wait()
    code = local_lists(place_ref, lists[...])
    list_row = lax.broadcasted_iota(jnp.int32, code.shape, 1)
    lane = lax.broadcasted_iota(jnp.int32, (code.shape[0], 128), 1)
    for b in range(blocks):
        wanted = place_ref[0] * blocks + b
        listed = jnp.sum(jnp.where(list_row == wanted, code, 0.0), axis=1, keepdims=True).astype(jnp.int32)
        slot = jnp.where(listed < 0, -1, lax.div(listed, 128))
        found = jnp.where(slot == lane, lax.rem(listed, 128), 0)
        phase = jnp.where(slot < 0, -1, lax.div(slot, WIDTH))
        found = found + jnp.where(phase == lane - COUNTS, jnp.where(phase < 0, 0, 1), 0)
        ids[b : b + 1, :] = jnp.sum(found.astype(F32), axis=0, keepdims=True).astype(jnp.int32)
    tell = pltpu.make_async_copy(ids, ids_smem, sems.at[len(moves)])
    tell.start()
    for copy in copies[1:]:
        copy.wait()
    wv_t[...] = wv[...].T
    proj = jnp.dot(queries[...], wq[...], preferred_element_type=F32).astype(BF16)
    head = head_of_lane((QBLK, D))
    scale = LOG2E / math.sqrt(HD)
    none = jnp.zeros((QBLK, D), BF16)
    for b in range(blocks):
        rows = proj[b * QBLK : (b + 1) * QBLK]
        for c in range(PAIRS):
            two = [jnp.where(head == h, rows, none) for h in (2 * c, 2 * c + 1)]
            folded = lax.dot_general(wk[...], jnp.concatenate(two, axis=0), NT, preferred_element_type=F32)
            out_ref[b, :, c * WIDE : (c + 1) * WIDE] = (folded * scale).astype(BF16)
    tell.wait()
    write_items(ids_smem, items, blocks)


def project(place, count, lists, queries, w_query, w_key, w_value, w_out, norm_gain, w_mask, features):
    blocks = queries.shape[0] // QBLK
    square = jax.ShapeDtypeStruct((D, D), BF16)
    gain = norm_gain.reshape(1, D)
    return pl.pallas_call(
        project_kernel,
        out_shape=(
            jax.ShapeDtypeStruct((blocks, D, H * QBLK), BF16),
            jax.ShapeDtypeStruct((8, 128), jnp.int32),
            square,
            square,
            jax.ShapeDtypeStruct(gain.shape, F32),
            square,
            jax.ShapeDtypeStruct(features.shape, BF16),
            jax.ShapeDtypeStruct((count, D), BF16),
        ),
        in_specs=[IN_SMEM] + [IN_HBM] * 9,
        out_specs=(IN_VMEM, IN_SMEM) + (IN_VMEM,) * 6,
        scratch_shapes=[
            pltpu.VMEM(lists.shape, jnp.int32),
            pltpu.VMEM(queries.shape, BF16),
            pltpu.VMEM((D, D), BF16),
            pltpu.VMEM((D, D), BF16),
            pltpu.VMEM((D, D), BF16),
            pltpu.VMEM((blocks, 128), jnp.int32),
            pltpu.SMEM((blocks, 128), jnp.int32),
            pltpu.SemaphoreType.DMA((11,)),
        ],
        compiler_params=pltpu.CompilerParams(vmem_limit_bytes=16 * MIB),
        cost_estimate=pl.CostEstimate(
            flops=2 * queries.shape[0] * D * D * (H + 1), bytes_accessed=3 * MIB, transcendentals=0
        ),
        name="project",
    )(place, *map(stay, (lists, queries, w_query, w_key, w_value, w_out, gain, w_mask, features)))


def keys_of(item, feats):
    rows = [lax.rem(lax.div(item, 16 * step), 64) * SBLK for step in (1, 64)]
    return jnp.concatenate([feats[pl.ds(pl.multiple_of(row, SBLK), SBLK), :] for row in rows], axis=0)


def score(item, feats, q_ref, scores):
    b = jnp.minimum(lax.rem(item, 16), q_ref.shape[0] - 1)
    scores[...] = jnp.dot(keys_of(item, feats), q_ref[b], preferred_element_type=F32)


def weigh(item, feats, scores, acc, stats):
    b = lax.rem(item, 16)
    turned = keys_of(item, feats).T
    alone = lax.div(item, 16 * 64 * 64) == 1
    halves = H * QBLK // 2
    for c in range(2):
        part = slice(c * halves, (c + 1) * halves)
        first = scores[:SBLK, part]
        second = jnp.where(alone, -jnp.inf, scores[SBLK:, part])
        top = stats[b, 0:1, part]
        higher = jnp.maximum(top, jnp.max(jnp.maximum(first, second), axis=0, keepdims=True))
        factor = jnp.exp2(top - higher)
        first = jnp.exp2(first - higher)
        second = jnp.exp2(second - higher)
        stats[b, 0:1, part] = higher
        stats[b, 1:2, part] = stats[b, 1:2, part] * factor + jnp.sum(first + second, axis=0, keepdims=True)
        weights = jnp.concatenate([first.astype(BF16), second.astype(BF16)], axis=0)
        acc[b, :, part] = acc[b, :, part] * factor + jnp.dot(turned, weights, preferred_element_type=F32)


def attend_kernel(phase, sizes, last, items, q_ref, *rest):
    count = len(sizes)
    piece_refs, rest = rest[:count], rest[count:]
    if phase:
        rest = rest[2:]
    if last:
        wv_t, acc, stats_ref, out_ref, feats, even, odd = rest
    else:
        acc, stats_ref, feats, even, odd = rest
    held = 0
    if count == 1:
        feats = piece_refs[0]
    else:
        for size, ref in zip(sizes, piece_refs):
            feats[held : held + size, :] = ref[...]
            held += size
    if phase == 0:
        acc[...] = jnp.zeros(acc.shape, F32)
        stats_ref[:, 0:1, :] = jnp.full((acc.shape[0], 1, H * QBLK), -jnp.inf, F32)
        stats_ref[:, 1:2, :] = jnp.zeros((acc.shape[0], 1, H * QBLK), F32)
    score(items[phase, 0], feats, q_ref, even)

    def two_items(i, carry):
        score(items[phase, 2 * i + 1], feats, q_ref, odd)
        weigh(items[phase, 2 * i], feats, even, acc, stats_ref)
        score(items[phase, 2 * i + 2], feats, q_ref, even)
        weigh(items[phase, 2 * i + 1], feats, odd, acc, stats_ref)
        return carry

    lax.fori_loop(0, lax.div(items[phase, LAST] + 1, 2), two_items, 0)
    if not last:
        return
    slot = lax.broadcasted_iota(jnp.int32, (16, WIDE), 0)
    column = lax.broadcasted_iota(jnp.int32, (QBLK, D + TAIL), 1)
    odd_head = jnp.where(column < D, lax.rem(lax.div(column, HD), 2), lax.rem(lax.div(column, 16), 2))
    empty = jnp.zeros((TAIL - 32, WIDE), F32)
    for b in range(q_ref.shape[0]):
        diagonal = []
        tail = jnp.zeros((16, WIDE), F32)
        for two in range(PAIRS // 2):
            part = slice(two * 2 * WIDE, (two + 1) * 2 * WIDE)
            total = stats_ref[b, 1:2, part]
            mean = (acc[b, :, part] * (1.0 / total)).astype(BF16)
            heads = slice(4 * HD * two, 4 * HD * (two + 1))
            values = jnp.dot(wv_t[heads, :], mean, preferred_element_type=F32)
            diagonal += [values[: 2 * HD, :WIDE], values[2 * HD :, WIDE:]]
            level = stats_ref[b, 0:1, part] + jnp.log(total) * LOG2E
            for piece in range(3):
                rounded = level.astype(BF16).astype(F32)
                level = level - rounded
                for k in range(2):
                    at = piece * PAIRS + 2 * two + k
                    tail = jnp.where(slot == at, rounded[:, k * WIDE : (k + 1) * WIDE], tail)
        turned = jnp.concatenate(diagonal + [tail, tail, empty], axis=0).T
        rows = jnp.where(odd_head == 1, turned[QBLK:], turned[:QBLK])
        out_ref[b * QBLK : (b + 1) * QBLK, :] = rows.astype(BF16)


def attend(phase, items, folded, arrays, state, wv_t):
    blocks = folded.shape[0]
    last = wv_t is not None
    sizes = [a.shape[0] for a in arrays]
    out_shape = [
        jax.ShapeDtypeStruct((blocks + 1, D, H * QBLK), F32),
        jax.ShapeDtypeStruct((blocks + 1, 8, H * QBLK), F32),
    ]
    args = [items, folded, *arrays]
    in_specs = [IN_SMEM, IN_VMEM] + [IN_VMEM] * len(arrays)
    scratch = [pltpu.VMEM((sum(sizes), D), BF16)] + [pltpu.VMEM((2 * SBLK, H * QBLK), F32)] * 2
    aliases = {}
    if phase:
        aliases = {len(args): 0, len(args) + 1: 1}
        args += list(state)
        in_specs += [IN_VMEM] * 2
    if last:
        args.append(wv_t)
        in_specs.append(IN_VMEM)
        out_shape.append(jax.ShapeDtypeStruct((blocks * QBLK, D + TAIL), BF16))
    return pl.pallas_call(
        functools.partial(attend_kernel, phase, sizes, last),
        out_shape=out_shape,
        in_specs=in_specs,
        out_specs=[IN_VMEM] * len(out_shape),
        input_output_aliases=aliases,
        scratch_shapes=scratch,
        compiler_params=pltpu.CompilerParams(vmem_limit_bytes=16 * MIB),
        cost_estimate=pl.CostEstimate(flops=1_000_000_000, bytes_accessed=4 * MIB, transcendentals=700_000),
        name="attend_%d" % phase,
    )(*args)


def finish_kernel(got_ref, queries, wo, gain, out_ref):
    sources, count, _ = got_ref.shape
    slot = lax.broadcasted_iota(jnp.int32, (TAIL, D), 0)
    pairs = H // 2
    head = 2 * lax.rem(slot, pairs) + lax.div(slot, 16)
    spread = (head == head_of_lane((TAIL, D))) & (lax.rem(slot, 16) < 3 * pairs) & (slot < 32)
    spread = jnp.where(spread, 1.0, 0.0).astype(BF16)
    tails = got_ref[:, :, D:].reshape(sources * count, TAIL)
    levels = jnp.dot(tails, spread, preferred_element_type=F32).reshape(sources, count, D)
    factors = jnp.exp2(levels - jnp.max(levels, axis=0, keepdims=True))
    mixed = jnp.sum(factors * got_ref[:, :, :D].astype(F32), axis=0)
    attended = (mixed / jnp.sum(factors, axis=0)).astype(BF16)
    rows = queries[...].astype(F32) + jnp.dot(attended, wo[...], preferred_element_type=F32)
    center = rows - jnp.mean(rows, axis=1, keepdims=True)
    variance = jnp.mean(center * center, axis=1, keepdims=True)
    updated = (center * lax.rsqrt(variance + 1e-05) * gain[...]).astype(BF16)
    for i in range(sources):
        out_ref[i] = updated


def finish(got, queries, w_out, norm_gain):
    sources, count, _ = got.shape
    return pl.pallas_call(
        finish_kernel,
        out_shape=jax.ShapeDtypeStruct((sources, count, D), BF16),
        in_specs=[IN_VMEM] * 4,
        out_specs=IN_VMEM,
        compiler_params=pltpu.CompilerParams(vmem_limit_bytes=16 * MIB),
        cost_estimate=pl.CostEstimate(flops=10_000_000, bytes_accessed=MIB, transcendentals=140_000),
        name="finish",
    )(got, queries, w_out, norm_gain)


STEP = 512
SLOTS = 8


def piece_row(place_ref, piece):
    ahead, other = piece
    chip, core = lax.div(place_ref[0], 2), lax.rem(place_ref[0], 2)
    chip = lax.rem(chip + jnp.where(core == 0, -ahead, ahead) + CHIPS, CHIPS)
    core = 1 - core if other else core
    return (chip * 2 + core) * (OWN_BLOCKS * SBLK)


def logits_kernel(pieces, place_ref, updated_ref, wm, *rest):
    count = len(pieces)
    piece_refs = rest[:count]
    updated_out, out_ref, embed, tiles, in_sems, out_sems = rest[count:]
    keep = pltpu.make_async_copy(updated_ref, updated_out, in_sems.at[0])
    keep.start()
    rows = jnp.dot(updated_ref[...], wm[...], preferred_element_type=F32).astype(BF16)
    embed[...] = rows * (1.0 / math.sqrt(D))
    stores = []
    for i, ref in enumerate(piece_refs):
        for row in range(0, ref.shape[0], STEP):
            slot = len(stores) % SLOTS
            if len(stores) >= SLOTS:
                stores[-SLOTS].wait()
            tiles[slot] = lax.dot_general(
                embed[...], ref[row : row + STEP, :], NT, preferred_element_type=F32
            )
            column = pl.multiple_of(piece_row(place_ref, pieces[i]) + row, STEP)
            stores.append(
                pltpu.make_async_copy(tiles.at[slot], out_ref.at[:, pl.ds(column, STEP)], out_sems.at[slot])
            )
            stores[-1].start()
    for store in stores[-SLOTS:]:
        store.wait()
    keep.wait()


def logits(place, updated, w_mask, pieces, arrays):
    count = updated.shape[0]
    shard = sum(a.shape[0] for a in arrays)
    return pl.pallas_call(
        functools.partial(logits_kernel, pieces),
        out_shape=(
            jax.ShapeDtypeStruct(updated.shape, BF16),
            jax.ShapeDtypeStruct((count, shard), F32),
        ),
        in_specs=[IN_SMEM, IN_VMEM, IN_VMEM] + [IN_VMEM] * len(arrays),
        out_specs=(IN_HBM, IN_HBM),
        scratch_shapes=[
            pltpu.VMEM((count, D), BF16),
            pltpu.VMEM((SLOTS, count, STEP), F32),
            pltpu.SemaphoreType.DMA((1,)),
            pltpu.SemaphoreType.DMA((SLOTS,)),
        ],
        compiler_params=pltpu.CompilerParams(vmem_limit_bytes=16 * MIB),
        cost_estimate=pl.CostEstimate(
            flops=2 * count * shard * D, bytes_accessed=20 * MIB, transcendentals=0
        ),
        name="logits",
    )(place, updated, w_mask, *arrays)


def shards(queries, features, block_lists, w_query, w_key, w_value, w_out, norm_gain, w_mask):
    space = lax.axis_size("space")
    place = jnp.stack([lax.axis_index("query"), lax.axis_index("space")]).astype(jnp.int32)
    ring = [(y * 2 + c, (y + 1 - 2 * c) % CHIPS * 2 + c) for y in range(CHIPS) for c in range(2)]
    back = [(to, source) for source, to in ring]
    cores = [(i, i ^ 1) for i in range(2 * CHIPS)]

    def send(rows, pairs):
        return lax.ppermute(rows, "query", pairs)

    came = send(features, ring)
    beside = send(features, cores)
    count = queries.shape[0] // space
    weights = (w_query, w_key, w_value, w_out, norm_gain, w_mask)
    folded, items, wv_t, w_out, norm_gain, w_mask, own, mine = project(
        place, count, block_lists.T, queries, *weights, features
    )
    later, folded = lax.optimization_barrier((features, folded))
    back_came = send(later, back)
    state = attend(0, items, folded, [own, beside], None, None)
    came, state = lax.optimization_barrier((came, tuple(state)))
    far = send(came, ring)
    near = [came, back_came, send(came, cores)]
    state = attend(1, items, folded, near, state, None)
    far, state = lax.optimization_barrier((far, tuple(state)))
    final = [far, send(back_came, cores), send(far, cores)]
    state = attend(2, items, folded, final[:2], state, None)
    partial = attend(3, items, folded, final[2:], state, wv_t)[2]

    got = lax.all_to_all(partial.reshape(space, count, D + TAIL), "space", 0, 0)
    rows = finish(got, mine, w_out, norm_gain)
    updated = lax.all_to_all(rows, "space", 0, 0).reshape(queries.shape)
    pieces = [(0, False), (0, True), (1, False), (-1, False), (-1, True), (2, False), (1, True), (2, True)]
    return logits(place, updated, w_mask, pieces, [own, beside, *near, *final])


def solution(mesh):
    placed = (P("query", None), P(("space", "query"), None), P(), P(), P(), P(), P(), P(), P())
    return jax.shard_map(
        shards,
        mesh=mesh,
        in_specs=placed,
        out_specs=(P("query", None), P("query", "space")),
        check_vma=False,
    )
```
